32 devices in a mesh: seq: 8 (over z, y), head: 4 (over x, core).
Axes of the slice: x: 2, y: 2, z: 4, core: 2. Of those that a mesh axis runs over, the one named last changes fastest.
Arguments:
- tokens: bfloat16 [3072, 4096], P('seq', 'head'), may hold values from -6 to 6
- norm_gain: float32 [4096], replicated, may hold values from 0.25 to 1.75
- w_in: bfloat16 [4096, 8, 2304], P('seq', 'head'), may hold values from -0.09375 to 0.09375
- w_dt: bfloat16 [4096, 128], P('seq', 'head'), may hold values from -0.09375 to 0.09375
- dt_bias: float32 [128], P('head'), may hold values from -3 to -1
- a_log: float32 [128], P('head'), may hold values from -11 to -1
- d_skip: float32 [128], P('head'), may hold values from 0.5 to 1.5
- conv_w: float32 [4, 8, 1280], P(None, 'head'), may hold values from -0.5 to 0.5
- conv_b: float32 [8, 1280], P('head'), may hold values from -0.5 to 0.5
- gate_gain: float32 [8, 1024], P('head'), may hold values from 0.25 to 1.75
- w_out: bfloat16 [8, 1024, 4096], P('head'), may hold values from -0.09375 to 0.09375
Outputs:
- mixed: bfloat16 [3072, 4096], P('seq', 'head')
The draws below stay inside these ranges and needn't reach their ends.
All inputs are finite; a program needn't handle non-finite values.
Results may differ from the reference program's by a relative error of at most 0.018.
Values may be sent and summed in bfloat16 or wider, within the bound.
No kernel may reach another device: no remote copies, remote signals or barrier semaphores. Data moves between devices by JAX's collectives and lax.ppermute only.
A program may use at most 128 MiB of HBM per device.

```python
import jax
import jax.numpy as jnp
from jax import lax

D = 4096
HEADS = 128
G = 8
P_SIZE = 64
N = 128
KERNEL = 4
STRETCH = 128
TOKENS = 3072
HG = 16


def draw_a_log(key, part):
    chooser, levels = jax.random.split(jax.random.fold_in(key, 17))
    slow_share = 0.5
    is_slow = jax.random.uniform(chooser, (HEADS,), jnp.float32) < slow_share
    position = jax.random.uniform(levels, (HEADS,), jnp.float32)
    low_slow = jnp.log(1.0 / TOKENS)
    high_slow = jnp.log(4.0 / TOKENS)
    low_fast = jnp.log(0.05)
    high_fast = jnp.log(0.2)
    slow_value = low_slow + position * (high_slow - low_slow)
    fast_value = low_fast + position * (high_fast - low_fast)
    return jnp.where(is_slow, slow_value, fast_value).astype(jnp.float32)


def with_spikes(drawn, key, source, target, parts, factor):
    def block_of(axis_at):
        return (jnp.arange(drawn.shape[axis_at]) // (drawn.shape[axis_at] // parts)).reshape((-1,) + (1,) * (drawn.ndim - 1 - axis_at))

    first = jax.random.permutation(key, parts)[block_of(target)]
    other_side = (block_of(target) + parts // 2) % parts
    return jnp.where((block_of(source) == first) | (block_of(source) == other_side), factor * drawn, drawn)


def block_levels(key, dims, cuts, smallest, largest):
    def one(axis_at, blocks):
        draws = jax.random.uniform(jax.random.fold_in(jax.random.fold_in(key, 6), axis_at), (blocks,), jnp.float32, smallest / len(cuts), largest / len(cuts))
        return jnp.repeat(jnp.exp(draws), dims[axis_at] // blocks).reshape((-1,) + (1,) * (len(dims) - axis_at - 1))

    loudness = one(*cuts[0])
    for cut in cuts[1:]:
        loudness = loudness * one(*cut)
    return loudness


def normal_values(own_key, dims, spread, most, shards=(), kind=jnp.bfloat16):
    factor_of = block_levels(own_key, dims, shards, -0.22, 0.18) if shards else 1.0
    values = jax.random.normal(own_key, dims, jnp.float32) * spread * factor_of
    return jnp.minimum(jnp.maximum(values, -most), most).astype(kind)


def bell_draw_with(rng, shape, scale, bound, cuts, heavy, held_as=jnp.bfloat16):
    result = scale * jax.random.normal(rng, shape, jnp.float32)
    if cuts:
        result = result * block_levels(rng, shape, cuts, -0.22, 0.18)
    return jnp.clip(with_spikes(result, jax.random.fold_in(rng, 3), *heavy), -bound, bound).astype(held_as)


def setup_inputs(seed: int = 0) -> dict:
    key_list = jax.random.split(jax.random.key(seed), 12)
    tokens = normal_values(key_list[0], (TOKENS, D), 1.0, 6.0, ((0, 8), (1, 4)))
    norm_gain = jnp.clip(1.0 + 0.15 * jax.random.normal(key_list[1], (D,), jnp.float32), 0.25, 1.75)
    w_in = normal_values(key_list[2], (D, G, 2 * HG * P_SIZE + 2 * N), D ** -0.5, 0.09375, ((0, 8), (1, 4)))
    w_dt = normal_values(key_list[3], (D, HEADS), D ** -0.5, 0.09375, ((0, 8), (1, 4)))
    dt_bias = jnp.clip(-3.0 + 2.0 * jax.random.uniform(key_list[4], (HEADS,), jnp.float32) ** block_levels(key_list[4], (HEADS,), ((0, 4),), -0.2, 0.2), -3.0, -1.0)
    a_log = draw_a_log(jax.random.fold_in(key_list[11], 71), 0)
    d_skip = jnp.clip(0.5 + 1.0 * jax.random.uniform(key_list[6], (HEADS,), jnp.float32) ** block_levels(key_list[6], (HEADS,), ((0, 4),), -0.2, 0.2), 0.5, 1.5)
    conv_w = jnp.clip(jax.random.uniform(key_list[7], (KERNEL, G, HG * P_SIZE + 2 * N), jnp.float32, -0.5, 0.5) * block_levels(key_list[7], (KERNEL, G, HG * P_SIZE + 2 * N), ((1, 4),), -0.4, 0.0), -0.5, 0.5)
    conv_b = jnp.clip(jax.random.uniform(key_list[8], (G, HG * P_SIZE + 2 * N), jnp.float32, -0.5, 0.5) * block_levels(key_list[8], (G, HG * P_SIZE + 2 * N), ((0, 4),), -0.4, 0.0), -0.5, 0.5)
    gate_gain = jnp.clip(1.0 + 0.15 * jax.random.normal(key_list[9], (G, HG * P_SIZE), jnp.float32), 0.25, 1.75)
    w_out = bell_draw_with(key_list[10], (G, HG * P_SIZE, D), (HEADS * P_SIZE) ** -0.5, 0.09375, ((0, 4),), (0, 2, 4, 2.0))
    return {"tokens": tokens, "norm_gain": norm_gain, "w_in": w_in, "w_dt": w_dt, "dt_bias": dt_bias, "a_log": a_log, "d_skip": d_skip, "conv_w": conv_w, "conv_b": conv_b, "gate_gain": gate_gain, "w_out": w_out}


EPS = 1e-05
HIGHEST = lax.Precision.HIGHEST

def normalize(values, gain):
    squares = lax.optimization_barrier(jnp.mean(values * values, axis=-1, keepdims=True))
    return values * lax.rsqrt(squares + EPS) * gain

def state_block(inputs, step_size, log_decay, in_map, out_map, block_len):
    length = inputs.shape[0]
    stretch_count = length // block_len
    head_count = inputs.shape[1]
    head_size = inputs.shape[2]
    state_size = in_map.shape[1]
    shaped = (inputs.reshape(stretch_count, block_len, head_count, head_size), step_size.reshape(stretch_count, block_len, head_count), log_decay.reshape(stretch_count, block_len, head_count), in_map.reshape(stretch_count, block_len, state_size), out_map.reshape(stretch_count, block_len, state_size))
    causal = jnp.arange(block_len)[:, None] >= jnp.arange(block_len)[None, :]

    def advance(state_now, pieces):
        stretch_in, stretch_step, stretch_log, stretch_b, stretch_c = pieces
        cumulative = jnp.cumsum(stretch_log, axis=0)
        gap_log = cumulative[:, None, :] - cumulative[None, :, :]
        decays = jnp.where(causal[:, :, None], jnp.exp(jnp.where(causal[:, :, None], gap_log, 0.0)), 0.0)
        scores = jnp.dot(stretch_c, stretch_b.T, preferred_element_type=jnp.float32)
        wide_c = stretch_c.astype(jnp.float32)
        wide_b = stretch_b.astype(jnp.float32)
        weights = scores[:, :, None] * decays * stretch_step[None, :, :]
        within = jnp.einsum('ijh,jhp->ihp', weights, stretch_in, precision=HIGHEST)
        across = jnp.exp(cumulative)[:, :, None] * jnp.einsum('in,hpn->ihp', wide_c, state_now, precision=HIGHEST)
        to_end = jnp.exp(cumulative[-1][None, :] - cumulative) * stretch_step
        fresh_state = jnp.einsum('jh,jhp,jn->hpn', to_end, stretch_in, wide_b, precision=HIGHEST)
        state_next = jnp.exp(cumulative[-1])[:, None, None] * state_now + fresh_state
        return (state_next, within + across)
    start_state = jnp.zeros((head_count, head_size, state_size), jnp.float32)
    final, outputs = lax.scan(advance, start_state, shaped)
    return (outputs.reshape(length, head_count, head_size), final)

def reference(tokens, norm_gain, w_in, w_dt, dt_bias, a_log, d_skip, conv_w, conv_b, gate_gain, w_out):
    group_width = HG * P_SIZE
    normed = normalize(tokens.astype(jnp.float32), norm_gain).astype(jnp.bfloat16)
    step_all = jax.nn.softplus(jnp.dot(normed, w_dt, preferred_element_type=jnp.float32) + dt_bias)
    rates = jnp.exp(a_log)

    def group_step(totals, group_index):
        weight = lax.dynamic_index_in_dim(w_in, group_index, 1, keepdims=False)
        projected = lax.optimization_barrier(jnp.dot(normed, weight, preferred_element_type=jnp.float32).astype(jnp.bfloat16))
        gate_raw = projected[:, :group_width].astype(jnp.float32)
        channels = projected[:, group_width:].astype(jnp.float32)
        taps = lax.dynamic_index_in_dim(conv_w, group_index, 1, keepdims=False)
        bias_row = lax.dynamic_index_in_dim(conv_b, group_index, 0, keepdims=False)
        padded = jnp.concatenate([jnp.zeros((KERNEL - 1, channels.shape[1]), jnp.float32), channels], axis=0)
        summed = bias_row[None, :]
        for offset in range(KERNEL):
            summed = summed + taps[offset][None, :] * padded[offset:offset + TOKENS]
        narrow = lax.optimization_barrier(jax.nn.silu(summed).astype(jnp.bfloat16))
        convolved = narrow.astype(jnp.float32)
        inputs = convolved[:, :group_width].reshape(TOKENS, HG, P_SIZE)
        in_map = narrow[:, group_width:group_width + N]
        out_map = narrow[:, group_width + N:]
        first = (group_index * HG).astype(jnp.int32)
        step_size = lax.dynamic_slice_in_dim(step_all, first, HG, 1)
        log_decay = -lax.dynamic_slice_in_dim(rates, first, HG, 0)[None, :] * step_size
        skip_row = lax.dynamic_slice_in_dim(d_skip, first, HG, 0)
        outputs, final = state_block(inputs, step_size, log_decay, in_map, out_map, STRETCH)
        outputs = outputs + skip_row[None, :, None] * inputs
        gated = outputs.reshape(TOKENS, group_width) * jax.nn.silu(gate_raw)
        gain_row = lax.dynamic_index_in_dim(gate_gain, group_index, 0, keepdims=False)
        normed_out = normalize(gated, gain_row).astype(jnp.bfloat16)
        out_rows = lax.dynamic_index_in_dim(w_out, group_index, 0, keepdims=False)
        return (totals + jnp.dot(normed_out, out_rows, preferred_element_type=jnp.float32), None)
    totals, unused = lax.scan(group_step, jnp.zeros((TOKENS, D), jnp.float32), jnp.arange(G, dtype=jnp.int32))
    return totals.astype(jnp.bfloat16)
```

```python
from functools import partial

import jax
import jax.numpy as jnp
from jax import lax
from jax.experimental import pallas as pl
from jax.experimental.pallas import tpu as pltpu
from jax.sharding import PartitionSpec as P

STRETCH = 128


EPS = 1e-05
HIGHEST = lax.Precision.HIGHEST
VMEM_LIMIT = 58 * 1024 * 1024
LANES = 128


def swap(value, axis, bit):
    count = lax.axis_size(axis)
    return lax.ppermute(value, axis, [(i, i ^ bit) for i in range(count)])


def after(values, *gates):
    return lax.optimization_barrier((values, gates))[0]


def silu_of(v):
    return v * (1.0 / (1.0 + jnp.exp(-v)))


def spread(columns, heads, width):
    rows = columns.shape[0]
    head_of = lax.broadcasted_iota(jnp.int32, (rows, heads * width), 1) // width
    out = jnp.broadcast_to(columns[:, heads - 1 : heads], (rows, heads * width))
    for j in range(heads - 2, -1, -1):
        out = jnp.where(head_of == j, columns[:, j : j + 1], out)
    return out


def mixer_kernel(
    cfg,
    where_ref,
    *refs,
):
    (shards, arrays, blocks, rows, feats, krows, heads, width, state_size, taps, dim) = cfg
    pieces = [[refs[a * blocks + e] for e in range(blocks)] for a in range(arrays)]
    at = arrays * blocks
    mains = refs[at : at + shards]
    maps = refs[at + shards : at + 2 * shards]
    (dt_w, conv_w, conv_b, dt_bias, neg_rate, skip, out_ref, wbuf, xbuf, pbuf, cbuf, state, wsem, xsem) = refs[
        at + 2 * shards :
    ]
    i = pl.program_id(0)
    steps = pl.num_programs(0)
    me_s, me_h = where_ref[0], where_ref[1]
    chans = heads * width
    conv_cols = chans + 2 * state_size
    main_cols = 2 * chans
    map_cols = 2 * state_size
    per = feats // krows

    def fetch(step, slot, start):
        which = where_ref[2 + step]
        for a in range(arrays):
            @pl.when(which == a)
            def _(a=a):
                for e in range(blocks):
                    copy = pltpu.make_async_copy(
                        pieces[a][e], xbuf.at[slot, :, pl.ds(e * feats, feats)], xsem.at[slot, e]
                    )
                    if start:
                        copy.start()
                    else:
                        copy.wait()

    def weights(start):
        for d in range(shards):
            kb = me_s ^ d
            row = ((kb // per) ^ me_h) * feats + (kb % per) * krows
            row = pl.multiple_of(row, krows)
            for n, (src, lo, cols) in enumerate(
                ((mains[d], 0, main_cols), (maps[d], main_cols, map_cols))
            ):
                copy = pltpu.make_async_copy(
                    src, wbuf.at[pl.ds(row, krows), pl.ds(lo, cols)], wsem.at[n, d]
                )
                if start:
                    copy.start()
                else:
                    copy.wait()
        for e in range(blocks):
            src_row = pl.multiple_of((me_h ^ e) * feats, feats)
            copy = pltpu.make_async_copy(
                dt_w.at[pl.ds(src_row, feats), :],
                wbuf.at[pl.ds(e * feats, feats), pl.ds(main_cols + map_cols, LANES)],
                wsem.at[2, e],
            )
            if start:
                copy.start()
            else:
                copy.wait()

    slot = lax.rem(i, 2)

    @pl.when(i == 0)
    def _():
        fetch(0, 0, True)
        weights(True)
        state[...] = jnp.zeros_like(state)
        cbuf[0:8, :] = jnp.zeros((8, conv_cols), jnp.float32)

    @pl.when(i + 1 < steps)
    def _():
        fetch(i + 1, 1 - slot, True)

    @pl.when(i == 0)
    def _():
        weights(False)

    fetch(i, slot, False)

    total = main_cols + map_cols + LANES
    squares = jnp.zeros((rows, 1), jnp.float32)
    for e in range(blocks):
        part = xbuf[slot, :, e * feats : (e + 1) * feats].astype(jnp.float32)
        squares = squares + jnp.sum(part * part, axis=1, keepdims=True)
    factor = lax.rsqrt(squares * (1.0 / dim) + EPS)
    lo = 0
    while lo < total:
        cols = min(256, total - lo)
        pbuf[:, lo : lo + cols] = (
            jnp.dot(xbuf[slot], wbuf[:, lo : lo + cols], preferred_element_type=jnp.float32) * factor
        )
        lo += cols
    cbuf[8 : 8 + rows, :] = pbuf[:, chans : chans + conv_cols].astype(jnp.bfloat16).astype(jnp.float32)

    length = STRETCH
    tri = lax.broadcasted_iota(jnp.int32, (length, length), 0) >= lax.broadcasted_iota(
        jnp.int32, (length, length), 1
    )
    ones = jnp.where(tri, 1.0, 0.0).astype(jnp.float32)
    lane_head = lax.broadcasted_iota(jnp.int32, (length, chans), 1) // width
    for st in range(rows // length):
        r0 = st * length
        summed = conv_b[...]
        for k in range(taps):
            first = 8 - (taps - 1) + k + r0
            summed = summed + conv_w[k : k + 1, :] * cbuf[first : first + length, :]
        narrow = silu_of(summed).astype(jnp.bfloat16)
        xin = narrow[:, :chans]
        in_map = narrow[:, chans : chans + state_size]
        out_map = narrow[:, chans + state_size :]
        xf = xin.astype(jnp.float32)
        raw = pbuf[r0 : r0 + length, total - LANES :] + dt_bias[...]
        step = jnp.maximum(raw, 0.0) + jnp.log1p(jnp.exp(-jnp.abs(raw)))
        logd = neg_rate[...] * step
        cum = jnp.dot(ones, logd, preferred_element_type=jnp.float32, precision=HIGHEST)
        last = cum[length - 1 : length, :]
        cum_t = cum.T
        step_t = step.T
        scores = lax.dot_general(
            out_map, in_map, (((1,), (1,)), ((), ())), preferred_element_type=jnp.float32
        )
        weighted, spaced = [], []
        for j in range(heads):
            gap = cum[:, j : j + 1] - cum_t[j : j + 1, :]
            decay = jnp.where(tri, jnp.exp(jnp.where(tri, gap, 0.0)), 0.0)
            weighted.append((scores * decay * step_t[j : j + 1, :]).astype(jnp.bfloat16))
            spaced.append(jnp.where(lane_head == j, xf, 0.0).astype(jnp.bfloat16))
        within = jnp.dot(
            jnp.concatenate(weighted, axis=1),
            jnp.concatenate(spaced, axis=0),
            preferred_element_type=jnp.float32,
        )
        now = state[...]
        across = jnp.dot(out_map, now.astype(jnp.bfloat16), preferred_element_type=jnp.float32)
        y = within + spread(jnp.exp(cum), heads, width) * across + skip[...] * xf
        to_end = spread(jnp.exp(last - cum) * step, heads, width)
        fresh = lax.dot_general(
            in_map,
            (xf * to_end).astype(jnp.bfloat16),
            (((0,), (0,)), ((), ())),
            preferred_element_type=jnp.float32,
        )
        state[...] = spread(jnp.exp(last), heads, width) * now + fresh
        gate = pbuf[r0 : r0 + length, :chans].astype(jnp.bfloat16).astype(jnp.float32)
        out_ref[r0 : r0 + length, :] = (y * silu_of(gate)).astype(jnp.bfloat16)
    cbuf[0:8, :] = cbuf[rows : rows + 8, :]


def mixer(where, pieces, mains, maps, dt_w, conv_w, conv_b, dt_bias, neg_rate, skip, rows, heads, width, dim):
    arrays, blocks, shards = len(pieces), len(pieces[0]), len(mains)
    feats = pieces[0][0].shape[1]
    krows = mains[0].shape[0]
    chans = heads * width
    state_size = maps[0].shape[1] // 2
    taps = conv_w.shape[0]
    total = 2 * chans + 2 * state_size + LANES
    cfg = (shards, arrays, blocks, rows, feats, krows, heads, width, state_size, taps, dim)
    hbm = pl.BlockSpec(memory_space=pl.ANY)

    def whole(a):
        return pl.BlockSpec(a.shape, lambda i, w: (0,) * a.ndim)

    small = (conv_w, conv_b, dt_bias, neg_rate, skip)
    flat = [p for row in pieces for p in row]
    return pl.pallas_call(
        partial(mixer_kernel, cfg),
        out_shape=jax.ShapeDtypeStruct((rows * shards, chans), jnp.bfloat16),
        grid_spec=pltpu.PrefetchScalarGridSpec(
            num_scalar_prefetch=1,
            grid=(shards,),
            in_specs=[hbm] * (len(flat) + 2 * shards + 1) + [whole(a) for a in small],
            out_specs=pl.BlockSpec((rows, chans), lambda i, w: (i, 0)),
            scratch_shapes=[
                pltpu.VMEM((dim, total), jnp.bfloat16),
                pltpu.VMEM((2, rows, dim), jnp.bfloat16),
                pltpu.VMEM((rows, total), jnp.float32),
                pltpu.VMEM((8 + rows, chans + 2 * state_size), jnp.float32),
                pltpu.VMEM((state_size, chans), jnp.float32),
                pltpu.SemaphoreType.DMA((3, max(shards, blocks))),
                pltpu.SemaphoreType.DMA((2, blocks)),
            ],
        ),
        compiler_params=pltpu.CompilerParams(vmem_limit_bytes=VMEM_LIMIT, dimension_semantics=("arbitrary",)),
        cost_estimate=pl.CostEstimate(
            flops=2 * rows * shards * dim * total, bytes_accessed=2 * rows * shards * dim, transcendentals=0
        ),
    )(where, *flat, *mains, *maps, dt_w, *small)


def out_kernel(cfg, where_ref, *refs):
    shards, chans, groups, order = cfg
    gated = refs[:shards]
    gain, w_ref, out_ref, flat = refs[shards:]
    me_s = where_ref[0]
    per = shards // groups

    @pl.when(pl.program_id(0) == 0)
    def _():
        for g in range(groups):
            squares = 0.0
            parts = []
            for d in range(g * per, (g + 1) * per):
                part = gated[d][...].astype(jnp.float32)
                parts.append(part)
                squares = squares + jnp.sum(part * part, axis=1, keepdims=True)
            factor = lax.rsqrt(squares * (1.0 / (per * chans)) + EPS)
            for d, part in zip(range(g * per, (g + 1) * per), parts):
                t = me_s ^ d
                value = (part * factor * gain[pl.ds(t, 1), :]).astype(jnp.bfloat16)
                flat[:, pl.ds(pl.multiple_of(t * chans, chans), chans)] = value

    out_ref[...] = jnp.dot(flat[...], w_ref[...], preferred_element_type=jnp.float32).astype(jnp.bfloat16)


def out_terms(where, gated, gain, w_flat, groups, blocks, order):
    shards = len(gated)
    rows, chans = gated[0].shape
    depth, dim = w_flat.shape
    feats = dim // blocks
    tile = min(512, feats)
    tiles = feats // tile

    def column(i, w):
        e = order[-1]
        for n in range(len(order) - 2, -1, -1):
            e = jnp.where(i // tiles == n, order[n], e)
        return (0, (w[1] ^ e) * tiles + lax.rem(i, tiles))

    return pl.pallas_call(
        partial(out_kernel, (shards, chans, groups, order)),
        out_shape=jax.ShapeDtypeStruct((rows, feats * len(order)), jnp.bfloat16),
        grid_spec=pltpu.PrefetchScalarGridSpec(
            num_scalar_prefetch=1,
            grid=(tiles * len(order),),
            in_specs=[pl.BlockSpec((rows, chans), lambda i, w: (0, 0))] * shards
            + [pl.BlockSpec(gain.shape, lambda i, w: (0, 0)), pl.BlockSpec((depth, tile), column)],
            out_specs=pl.BlockSpec((rows, tile), lambda i, w: (0, i)),
            scratch_shapes=[pltpu.VMEM((rows, depth), jnp.bfloat16)],
        ),
        compiler_params=pltpu.CompilerParams(vmem_limit_bytes=VMEM_LIMIT, dimension_semantics=("arbitrary",)),
        cost_estimate=pl.CostEstimate(
            flops=2 * rows * depth * feats * len(order),
            bytes_accessed=2 * depth * feats * len(order),
            transcendentals=0,
        ),
    )(where, *gated, gain, w_flat)


def gather_tokens(tokens):
    outer = lax.axis_size("seq") // 2
    half = outer // 2
    at = lax.axis_index("seq") // 2

    def line(value, pairs):
        return lax.ppermute(value, "seq", [(2 * a + y, 2 * b + y) for a, b in pairs for y in (0, 1)])

    near = swap(tokens, "seq", 2)
    crossing = [line(v, [(1, 2), (2, 1)]) for v in (tokens, near)]
    outward = [line(v, [(1, 0), (2, 3)]) for v in crossing]
    middle = (at == 1) | (at == 2)
    far = [jnp.where(middle, a, b) for a, b in zip(crossing, outward)]
    rows = [tokens, near, *far]
    both = []
    for value in rows:
        both += [value, swap(value, "seq", 1)]
    pairs = [(v, swap(v, "head", 2)) for v in both]
    pieces = [(a, swap(a, "head", 1), b, swap(b, "head", 1)) for a, b in pairs]
    return pieces, far


def piece_table(shards):
    me = lax.axis_index("seq")
    shard = jnp.arange(shards)
    outer = (shard // 2) ^ (me // 2)
    middle = (me // 2 == 1) | (me // 2 == 2)
    slot = jnp.where((outer >= 2) & middle, outer ^ 1, outer)
    return slot * 2 + ((shard ^ me) & 1)


def head_split_body(
    tokens, norm_gain, w_in, w_dt, dt_bias, a_log, d_skip, conv_w, conv_b, gate_gain, w_out
):
    shards, blocks = lax.axis_size("seq"), lax.axis_size("head")
    s, h = lax.axis_index("seq"), lax.axis_index("head")
    rows = tokens.shape[0]
    krows, groups, wide = w_in.shape
    group_width = gate_gain.shape[1]
    state_size = (conv_b.shape[1] - group_width) // 2
    local_heads = dt_bias.shape[0]
    heads = local_heads // shards
    width = groups * group_width // local_heads
    chans = heads * width
    per = shards // groups
    dim = krows * shards

    pieces, far = gather_tokens(tokens)

    gain = lax.dynamic_slice_in_dim(norm_gain, s * krows, krows, 0)

    def columns(t, first, count):
        part = lax.dynamic_slice(w_in, (0, t // per, first), (krows, 1, count))[:, 0]
        return (part.astype(jnp.float32) * gain[:, None]).astype(jnp.bfloat16)

    to_send = []
    for d in range(shards):
        t = s ^ d
        first = (t % per) * chans
        to_send.append(
            jnp.concatenate([columns(t, first, chans), columns(t, group_width + first, chans)], axis=1)
        )
    far_map = columns(s ^ per, 2 * group_width, 2 * state_size)
    own_map = columns(s, 2 * group_width, 2 * state_size)
    dt_w = lax.all_gather(
        (w_dt.astype(jnp.float32) * gain[:, None]).astype(jnp.bfloat16), "seq", axis=0, tiled=True
    )
    dt_w = lax.dynamic_slice_in_dim(dt_w, s * heads, heads, 1)
    dt_w = jnp.pad(dt_w, ((0, 0), (0, LANES - heads)))
    to_send, far_map = after((to_send, far_map), *far)
    maps = [own_map] + [None] * (shards - 1)
    maps[per] = swap(far_map, "seq", per)
    bit = per // 2
    while bit:
        for d in [d for d in range(shards) if maps[d] is not None]:
            if not d & bit and maps[d | bit] is None:
                maps[d | bit] = swap(maps[d], "seq", bit)
        bit //= 2
    mains = [to_send[0]] + [None] * (shards - 1)
    for d in range(shards - 1, 0, -1):
        mains[d] = swap(to_send[d], "seq", d)

    group = s // per
    quarter = (s % per) * chans

    def own_channels(a):
        a = lax.dynamic_index_in_dim(a, group, a.ndim - 2, keepdims=False)
        inputs = lax.dynamic_slice_in_dim(a, quarter, chans, a.ndim - 1)
        return jnp.concatenate([inputs, a[..., group_width:]], axis=-1)

    def own_heads(a):
        return lax.dynamic_slice_in_dim(a, s * heads, heads, 0)

    def lanes(a):
        return jnp.pad(a, (0, LANES - heads))[None, :]

    where = jnp.concatenate([jnp.stack([s, h]), piece_table(shards)]).astype(jnp.int32)
    gated = mixer(
        where,
        pieces,
        mains,
        maps,
        dt_w,
        own_channels(conv_w),
        own_channels(conv_b)[None, :],
        lanes(own_heads(dt_bias)),
        lanes(-jnp.exp(own_heads(a_log))),
        jnp.repeat(own_heads(d_skip), width)[None, :],
        rows,
        heads,
        width,
        dim,
    )
    blocks_out = [
        lax.dynamic_slice_in_dim(gated, (s ^ d) * rows, rows, 0) for d in range(shards)
    ]
    arrived = [blocks_out[0]] + [None] * (shards - 1)
    for d in range(shards - 1, 0, -1):
        arrived[d] = swap(blocks_out[d], "seq", d)

    gains = gate_gain.reshape(shards, chans)
    w_flat = w_out.reshape(groups * group_width, w_out.shape[2])
    feats = w_flat.shape[1] // blocks
    lead = out_terms(where, arrived, gains, w_flat, groups, blocks, (3, 1))
    other = swap(lead, "head", 1)
    own = out_terms(where, arrived, gains, w_flat, groups, blocks, (2, 0))
    wide_sum = own.astype(jnp.float32) + other.astype(jnp.float32)
    beyond = swap(wide_sum[:, :feats].astype(jnp.bfloat16), "head", 2)
    return (wide_sum[:, feats:] + beyond.astype(jnp.float32)).astype(jnp.bfloat16)


def fits_head_split(mesh, w_in, gate_gain, dt_bias):
    shards, blocks = mesh.shape["seq"], mesh.shape["head"]
    groups = gate_gain.shape[0] // blocks
    local_heads = dt_bias.shape[0] // blocks
    chans = groups * gate_gain.shape[1] // shards
    return shards == 8 and blocks == 4 and groups == 2 and local_heads % shards == 0 and chans % LANES == 0


def from_behind(shard, axis, by):
    count = lax.axis_size(axis)
    pairs = [(i, i + by) for i in range(count) if 0 <= i + by < count]
    return lax.ppermute(shard, axis, pairs)


def carried_in(shard, axis, combine, identity):
    count, index = (lax.axis_size(axis), lax.axis_index(axis))
    everything = jax.tree.map(
        lambda part, kind: lax.all_gather(part.astype(kind), axis),
        shard,
        (jnp.bfloat16, jnp.bfloat16),
    )
    start = jax.tree.map(
        lambda part, zero: jnp.broadcast_to(jnp.asarray(zero, part.dtype), part.shape),
        shard,
        identity,
    )

    def lap(k, before):
        reached = k < index
        new = combine(
            before, jax.tree.map(lambda part, own: part[k].astype(own.dtype), everything, shard)
        )
        return jax.tree.map(lambda a, b: jnp.where(reached, a, b), new, before)

    return lax.fori_loop(0, count, lap, start)


def normalize(values, gain):
    squares = jnp.mean(values * values, axis=-1, keepdims=True)
    return values * lax.rsqrt(squares + EPS) * gain


def state_block(inputs, step_size, log_decay, in_map, out_map, block_len):
    length = inputs.shape[0]
    stretch_count = length // block_len
    head_count = inputs.shape[1]
    head_size = inputs.shape[2]
    state_size = in_map.shape[1]
    shaped = (
        inputs.reshape(stretch_count, block_len, head_count, head_size),
        step_size.reshape(stretch_count, block_len, head_count),
        log_decay.reshape(stretch_count, block_len, head_count),
        in_map.reshape(stretch_count, block_len, state_size),
        out_map.reshape(stretch_count, block_len, state_size),
    )
    causal = jnp.arange(block_len)[:, None] >= jnp.arange(block_len)[None, :]

    def advance(state_now, pieces):
        stretch_in, stretch_step, stretch_log, stretch_b, stretch_c = pieces
        cumulative = jnp.cumsum(stretch_log, axis=0)
        gap_log = cumulative[:, None, :] - cumulative[None, :, :]
        decays = jnp.where(
            causal[:, :, None], jnp.exp(jnp.where(causal[:, :, None], gap_log, 0.0)), 0.0
        )
        scores = jnp.dot(stretch_c, stretch_b.T, preferred_element_type=jnp.float32)
        wide_c = stretch_c.astype(jnp.float32)
        wide_b = stretch_b.astype(jnp.float32)
        weights = scores[:, :, None] * decays * stretch_step[None, :, :]
        within = jnp.einsum("ijh,jhp->ihp", weights, stretch_in, precision=HIGHEST)
        across = jnp.exp(cumulative)[:, :, None] * jnp.einsum(
            "in,hpn->ihp", wide_c, state_now, precision=HIGHEST
        )
        to_end = jnp.exp(cumulative[-1][None, :] - cumulative) * stretch_step
        fresh_state = jnp.einsum("jh,jhp,jn->hpn", to_end, stretch_in, wide_b, precision=HIGHEST)
        state_next = jnp.exp(cumulative[-1])[:, None, None] * state_now + fresh_state
        return (state_next, within + across)

    start_state = jnp.zeros((head_count, head_size, state_size), jnp.float32)
    final, outputs = lax.scan(advance, start_state, shaped)
    return (outputs.reshape(length, head_count, head_size), final)


def link_states(earlier, later):
    return (earlier[0] + later[0], jnp.exp(later[0])[:, :, None, None] * earlier[1] + later[1])


def sequence_split_body(tokens, norm_gain, w_in, w_dt, dt_bias, a_log, d_skip, conv_w, conv_b, gate_gain, w_out):
    local_rows = tokens.shape[0]
    kernel_len = conv_w.shape[0]
    groups, group_width = gate_gain.shape
    head_count = dt_bias.shape[0]
    per_group = head_count // groups
    head_size = group_width // per_group
    state_size = (conv_b.shape[1] - group_width) // 2
    gathered = lax.all_gather(tokens, "head", axis=1, tiled=True)
    normed = normalize(gathered.astype(jnp.float32), norm_gain).astype(jnp.bfloat16)
    span_rows = normed.shape[0]
    flat_in = w_in.reshape(w_in.shape[0], groups * w_in.shape[2])
    proj_sum = jnp.dot(
        normed,
        lax.all_gather(flat_in, "seq", axis=0, tiled=True),
        preferred_element_type=jnp.float32,
    )
    step_sum = jnp.dot(
        normed, lax.all_gather(w_dt, "seq", axis=0, tiled=True), preferred_element_type=jnp.float32
    )
    projected = proj_sum.astype(jnp.bfloat16).reshape(span_rows, groups, w_in.shape[2])
    step_size = jax.nn.softplus(step_sum + dt_bias[None, :])
    gate_raw = projected[span_rows - local_rows :, :, :group_width]
    own_channels = projected[:, :, group_width:]
    rim_rows = from_behind(own_channels[local_rows - kernel_len + 1 :], "seq", 1)
    extended = jnp.concatenate([rim_rows, own_channels], axis=0)
    summed = conv_b[None, :, :]
    for offset in range(kernel_len):
        summed = summed + conv_w[offset][None, :, :] * extended[
            offset : offset + local_rows
        ].astype(jnp.float32)
    narrow = lax.optimization_barrier(jax.nn.silu(summed).astype(jnp.bfloat16))
    convolved = narrow.astype(jnp.float32)
    inputs = convolved[:, :, :group_width].reshape(local_rows, groups, per_group, head_size)
    in_map = narrow[:, :, group_width : group_width + state_size]
    out_map = narrow[:, :, group_width + state_size :]
    step_grouped = step_size.reshape(local_rows, groups, per_group)
    log_decay = -jnp.exp(a_log).reshape(groups, per_group)[None, :, :] * step_grouped
    run_block = jax.vmap(
        partial(state_block, block_len=STRETCH), in_axes=(1, 1, 1, 1, 1), out_axes=(1, 0)
    )
    local_out, ending = run_block(inputs, step_grouped, log_decay, in_map, out_map)
    totals = jnp.sum(log_decay, axis=0)
    identity = (jnp.zeros_like(totals), jnp.zeros_like(ending))
    prior_decay, incoming = carried_in((totals, ending), "seq", link_states, identity)
    cumulative = jnp.exp(jnp.cumsum(log_decay, axis=0))
    carried = (
        jnp.einsum("tgn,ghpn->tghp", out_map.astype(jnp.float32), incoming, precision=HIGHEST)
        * cumulative[:, :, :, None]
    )
    outputs = local_out + carried + d_skip.reshape(groups, per_group)[None, :, :, None] * inputs
    gated = outputs.reshape(local_rows, groups, group_width) * jax.nn.silu(
        gate_raw.astype(jnp.float32)
    )
    normed_out = normalize(gated, gate_gain[None, :, :]).astype(jnp.bfloat16)
    flat_out = normed_out.reshape(local_rows, groups * group_width)
    terms = jnp.dot(
        flat_out,
        w_out.reshape(groups * group_width, w_out.shape[2]),
        preferred_element_type=jnp.float32,
    )
    return lax.psum_scatter(terms.astype(jnp.bfloat16), "head", scatter_dimension=1, tiled=True)


def solution(mesh):
    in_specs = (
        P("seq", "head"),
        P(),
        P("seq", "head", None),
        P("seq", "head"),
        P("head"),
        P("head"),
        P("head"),
        P(None, "head", None),
        P("head", None),
        P("head", None),
        P("head", None, None),
    )
    out_specs = P("seq", "head")

    def mixer_prefill(*args):
        by_heads = fits_head_split(mesh, args[2], args[9], args[4])
        body = head_split_body if by_heads else sequence_split_body
        mapped = jax.shard_map(
            body, mesh=mesh, in_specs=in_specs, out_specs=out_specs, check_vma=False
        )
        return mapped(*args)

    return mixer_prefill
```

```python
from functools import partial

import jax
import jax.numpy as jnp
from jax import lax
from jax.experimental import pallas as pl
from jax.experimental.pallas import tpu as pltpu
from jax.sharding import PartitionSpec as P

STRETCH = 128


EPS = 1e-05
HIGHEST = lax.Precision.HIGHEST
VMEM_LIMIT = 58 * 1024 * 1024
OUT_VMEM = 58 * 1024 * 1024
LANES = 128


def swap(value, axis, bit):
    count = lax.axis_size(axis)
    return lax.ppermute(value, axis, [(i, i ^ bit) for i in range(count)])


def silu_of(v):
    return v * (1.0 / (1.0 + jnp.exp(-v)))


def spread(columns, heads, width):
    rows = columns.shape[0]
    head_of = lax.broadcasted_iota(jnp.int32, (rows, heads * width), 1) // width
    out = jnp.broadcast_to(columns[:, heads - 1 : heads], (rows, heads * width))
    for j in range(heads - 2, -1, -1):
        out = jnp.where(head_of == j, columns[:, j : j + 1], out)
    return out


def mixer_kernel(
    cfg,
    where_ref,
    *refs,
):
    (shards, maps_of, blocks, rows, feats, krows, heads, width, state_size, taps, dim) = cfg
    many = shards - 1
    gathered, last = refs[:many], refs[many : many + 2]
    mains = refs[many + 2 : many + 2 + shards]
    (map_a, map_b, dt_w, conv_w, conv_b, dt_bias, neg_rate, skip) = refs[many + 2 + shards : many + 10 + shards]
    (out_ref, wbuf, xbuf, pbuf, pnext, cbuf, state, wsem, xsem) = refs[many + 10 + shards :]
    i = pl.program_id(0)
    steps = pl.num_programs(0)
    me_s, me_h = where_ref[0], where_ref[1]
    chans = heads * width
    conv_cols = chans + 2 * state_size
    main_cols = 2 * chans
    map_cols = 2 * state_size
    per = feats // krows
    dt_order = range(shards)

    def move(copy, start):
        if start:
            copy.start()
        else:
            copy.wait()

    def fetch(step, slot, start):
        which = where_ref[2 + step]
        for k in range(shards // 2):
            for inner in (0, 1):
                @pl.when(which == 2 * k + inner)
                def _(k=k, inner=inner):
                    part = pl.ds(inner * rows, rows)
                    for e in range(blocks):
                        beyond, core = divmod(e, 2)
                        array = k + beyond * (shards // 2)
                        if array < many:
                            src, block = gathered[array].at[core, part, :], e
                        else:
                            src, block = last[core].at[part, :], (e & ~1) + ((me_h & 1) ^ core)
                        dst = xbuf.at[slot, :, pl.ds(pl.multiple_of(block * feats, feats), feats)]
                        move(pltpu.make_async_copy(src, dst, xsem.at[slot, e]), start)

    def weights(start):
        for d in range(shards):
            kb = me_s ^ d
            block = kb // per
            place = ((block // 2) ^ (me_h // 2)) * 2 + (block % 2)
            row = pl.multiple_of(place * feats + (kb % per) * krows, krows)
            source, lo_row = maps_of[d]
            map_src = (map_a, map_b)[source].at[pl.ds(lo_row, krows), :]
            for n, (src, lo, cols) in enumerate(
                (
                    (mains[d], 0, main_cols),
                    (map_src, main_cols, map_cols),
                    (dt_w.at[dt_order[d]], main_cols + map_cols, LANES),
                )
            ):
                dst = wbuf.at[pl.ds(row, krows), pl.ds(lo, cols)]
                move(pltpu.make_async_copy(src, dst, wsem.at[n, d]), start)

    slot = lax.rem(i, 2)
    shard_count = steps - 1

    @pl.when(i == 0)
    def _():
        fetch(0, 0, True)
        weights(True)
        state[...] = jnp.zeros_like(state)
        cbuf[0:8, :] = jnp.zeros((8, conv_cols), jnp.float32)

    @pl.when(i + 1 < shard_count)
    def _():
        fetch(i + 1, 1 - slot, True)

    @pl.when(i == 0)
    def _():
        weights(False)

    @pl.when(i < shard_count)
    def _():
        fetch(i, slot, False)

    total = main_cols + map_cols + LANES
    tiles = [(lo, min(256, total - lo)) for lo in range(0, total, 256)]
    length = STRETCH
    stretches = rows // length

    def row_factor():
        squares = jnp.zeros((rows, 1), jnp.float32)
        for e in range(blocks):
            part = xbuf[slot, :, e * feats : (e + 1) * feats].astype(jnp.float32)
            squares = squares + jnp.sum(part * part, axis=1, keepdims=True)
        return lax.rsqrt(squares * (1.0 / dim) + EPS)

    def project(tile, factor):
        lo, cols = tile
        pnext[:, lo : lo + cols] = (
            jnp.dot(xbuf[slot], wbuf[:, lo : lo + cols], preferred_element_type=jnp.float32) * factor
        )

    def hand_over():
        pbuf[...] = pnext[...]
        cbuf[8 : 8 + rows, :] = pnext[:, chans : chans + conv_cols].astype(jnp.bfloat16).astype(jnp.float32)

    def constants():
        tri = lax.broadcasted_iota(jnp.int32, (length, length), 0) >= lax.broadcasted_iota(
            jnp.int32, (length, length), 1
        )
        ones = jnp.where(tri, 1.0, 0.0).astype(jnp.float32)
        lane_head = lax.broadcasted_iota(jnp.int32, (length, chans), 1) // width
        return tri, ones, lane_head

    def scan(st, tri, ones, lane_head):
        r0 = st * length
        summed = conv_b[...]
        for k in range(taps):
            first = 8 - (taps - 1) + k + r0
            summed = summed + conv_w[k : k + 1, :] * cbuf[first : first + length, :]
        narrow = silu_of(summed).astype(jnp.bfloat16)
        xin = narrow[:, :chans]
        in_map = narrow[:, chans : chans + state_size]
        out_map = narrow[:, chans + state_size :]
        xf = xin.astype(jnp.float32)
        raw = pbuf[r0 : r0 + length, total - LANES :] + dt_bias[...]
        step = jnp.maximum(raw, 0.0) + jnp.log1p(jnp.exp(-jnp.abs(raw)))
        logd = neg_rate[...] * step
        cum = jnp.dot(ones, logd, preferred_element_type=jnp.float32, precision=HIGHEST)
        last_row = cum[length - 1 : length, :]
        cum_t = cum.T
        step_t = step.T
        scores = lax.dot_general(
            out_map, in_map, (((1,), (1,)), ((), ())), preferred_element_type=jnp.float32
        )
        weighted, spaced = [], []
        for j in range(heads):
            gap = cum[:, j : j + 1] - cum_t[j : j + 1, :]
            decay = jnp.where(tri, jnp.exp(jnp.where(tri, gap, 0.0)), 0.0)
            weighted.append((scores * decay * step_t[j : j + 1, :]).astype(jnp.bfloat16))
            spaced.append(jnp.where(lane_head == j, xf, 0.0).astype(jnp.bfloat16))
        within = jnp.dot(
            jnp.concatenate(weighted, axis=1),
            jnp.concatenate(spaced, axis=0),
            preferred_element_type=jnp.float32,
        )
        now = state[...]
        across = jnp.dot(out_map, now.astype(jnp.bfloat16), preferred_element_type=jnp.float32)
        y = within + spread(jnp.exp(cum), heads, width) * across + skip[...] * xf
        to_end = spread(jnp.exp(last_row - cum) * step, heads, width)
        fresh = lax.dot_general(
            in_map,
            (xf * to_end).astype(jnp.bfloat16),
            (((0,), (0,)), ((), ())),
            preferred_element_type=jnp.float32,
        )
        state[...] = spread(jnp.exp(last_row), heads, width) * now + fresh
        gate = pbuf[r0 : r0 + length, :chans].astype(jnp.bfloat16).astype(jnp.float32)
        out_ref[r0 : r0 + length, :] = (y * silu_of(gate)).astype(jnp.bfloat16)

    def keep_tail():
        cbuf[0:8, :] = cbuf[rows : rows + 8, :]

    @pl.when(i == 0)
    def _():
        factor = row_factor()
        for tile in tiles:
            project(tile, factor)
        hand_over()

    @pl.when((i > 0) & (i < shard_count))
    def _():
        held = constants()
        factor = row_factor()
        for n in range(max(len(tiles), stretches)):
            if n < len(tiles):
                project(tiles[n], factor)
            if n < stretches:
                scan(n, *held)
        keep_tail()
        hand_over()

    @pl.when(i == shard_count)
    def _():
        held = constants()
        for n in range(stretches):
            scan(n, *held)


def mixer(
    where, gathered, last, mains, maps, maps_of, dt_w, conv_w, conv_b, dt_bias, neg_rate, skip, rows, heads, width, dim
):
    shards = len(mains)
    feats = last[0].shape[1]
    blocks = dim // feats
    krows = mains[0].shape[0]
    chans = heads * width
    state_size = maps[0].shape[1] // 2
    taps = conv_w.shape[0]
    total = 2 * chans + 2 * state_size + LANES
    cfg = (shards, tuple(maps_of), blocks, rows, feats, krows, heads, width, state_size, taps, dim)
    hbm = pl.BlockSpec(memory_space=pl.ANY)

    def whole(a):
        return pl.BlockSpec(a.shape, lambda i, w: (0,) * a.ndim)

    small = (conv_w, conv_b, dt_bias, neg_rate, skip)
    large = (*gathered, *last, *mains, *maps, dt_w)
    return pl.pallas_call(
        partial(mixer_kernel, cfg),
        out_shape=jax.ShapeDtypeStruct((rows * shards, chans), jnp.bfloat16),
        grid_spec=pltpu.PrefetchScalarGridSpec(
            num_scalar_prefetch=1,
            grid=(shards + 1,),
            in_specs=[hbm] * len(large) + [whole(a) for a in small],
            out_specs=pl.BlockSpec((rows, chans), lambda i, w: (jnp.maximum(i - 1, 0), 0)),
            scratch_shapes=[
                pltpu.VMEM((dim, total), jnp.bfloat16),
                pltpu.VMEM((2, rows, dim), jnp.bfloat16),
                pltpu.VMEM((rows, total), jnp.float32),
                pltpu.VMEM((rows, total), jnp.float32),
                pltpu.VMEM((8 + rows, chans + 2 * state_size), jnp.float32),
                pltpu.VMEM((state_size, chans), jnp.float32),
                pltpu.SemaphoreType.DMA((3, max(shards, blocks))),
                pltpu.SemaphoreType.DMA((2, blocks)),
            ],
        ),
        compiler_params=pltpu.CompilerParams(vmem_limit_bytes=VMEM_LIMIT, dimension_semantics=("arbitrary",)),
        cost_estimate=pl.CostEstimate(
            flops=2 * rows * shards * dim * total, bytes_accessed=2 * rows * shards * dim, transcendentals=0
        ),
    )(where, *large, *small)


def normed_terms_kernel(cfg, where_ref, *refs):
    shards, chans, groups = cfg
    gated = refs[:shards]
    gain, w_ref, out_ref, flat = refs[shards:]
    me_s = where_ref[0]
    per = shards // groups

    @pl.when(pl.program_id(0) == 0)
    def _():
        for g in range(groups):
            squares = 0.0
            parts = []
            for d in range(g * per, (g + 1) * per):
                part = gated[d][...].astype(jnp.float32)
                parts.append(part)
                squares = squares + jnp.sum(part * part, axis=1, keepdims=True)
            factor = lax.rsqrt(squares * (1.0 / (per * chans)) + EPS)
            for d, part in zip(range(g * per, (g + 1) * per), parts):
                t = me_s ^ d
                value = (part * factor * gain[pl.ds(t, 1), :]).astype(jnp.bfloat16)
                flat[:, pl.ds(pl.multiple_of(t * chans, chans), chans)] = value

    out_ref[...] = jnp.dot(flat[...], w_ref[...], preferred_element_type=jnp.float32).astype(jnp.bfloat16)


def terms_kernel(where_ref, flat, w_ref, out_ref):
    out_ref[...] = jnp.dot(flat[...], w_ref[...], preferred_element_type=jnp.float32).astype(jnp.bfloat16)


def out_terms(kernel, where, values, w_flat, rows, blocks, e, keep):
    depth, dim = w_flat.shape
    feats = dim // blocks
    tile = min(256, feats)
    tiles = feats // tile
    out_shape = jax.ShapeDtypeStruct((rows, feats), jnp.bfloat16)
    out_spec = pl.BlockSpec((rows, tile), lambda i, w: (0, i))
    if keep:
        out_shape = (out_shape, jax.ShapeDtypeStruct((rows, depth), jnp.bfloat16))
        out_spec = (out_spec, pl.BlockSpec((rows, depth), lambda i, w: (0, 0)))
    return pl.pallas_call(
        kernel,
        out_shape=out_shape,
        grid_spec=pltpu.PrefetchScalarGridSpec(
            num_scalar_prefetch=1,
            grid=(tiles,),
            in_specs=[pl.BlockSpec(v.shape, lambda i, w: (0, 0)) for v in values]
            + [pl.BlockSpec((depth, tile), lambda i, w: (0, (w[1] ^ e) * tiles + i))],
            out_specs=out_spec,
        ),
        compiler_params=pltpu.CompilerParams(vmem_limit_bytes=OUT_VMEM, dimension_semantics=("arbitrary",)),
        cost_estimate=pl.CostEstimate(
            flops=2 * rows * depth * feats, bytes_accessed=2 * depth * feats, transcendentals=0
        ),
    )(where, *values, w_flat)


def line(value, pairs):
    return lax.ppermute(value, "seq", [(2 * a + y, 2 * b + y) for a, b in pairs for y in (0, 1)])


def stack(*parts):
    return jnp.concatenate(parts, axis=0)


def both_cores(value):
    pairs = [[i, i + 1] for i in range(0, lax.axis_size("head"), 2)]
    return lax.all_gather(value, "head", axis=0, axis_index_groups=pairs)


def together(*values):
    return lax.optimization_barrier(values)


def exchange(tokens, main, far_map, own_map, dt_rows):
    at = lax.axis_index("seq") // 2
    middle = (at == 1) | (at == 2)
    cross, outward = [(1, 2), (2, 1)], [(1, 0), (2, 3)]

    def x_swap(v):
        return swap(v, "head", 2)

    def s_swap(v, bit):
        return swap(v, "seq", bit)

    xp, y0, z1, c0, dt_y, main, far_map, own_map = together(
        x_swap(tokens),
        s_swap(tokens, 1),
        s_swap(tokens, 2),
        line(tokens, cross),
        s_swap(dt_rows, 1),
        main,
        far_map,
        own_map,
    )
    dt_rows = stack(dt_rows, dt_y)
    xy, yz1, c1, o0, dt_z = together(
        x_swap(y0), s_swap(z1, 1), line(z1, cross), line(c0, outward), s_swap(dt_rows, 2)
    )
    dt_rows = stack(dt_rows, dt_z)
    q1 = jnp.where(middle, c0, o0)
    q1, z1, yz1, c1, far_map, dt_rows, m7 = together(q1, z1, yz1, c1, far_map, dt_rows, main[7])
    a1 = stack(z1, yz1)
    xa1, w7, yq1, o1, far_map, dt_far = together(
        x_swap(a1), s_swap(m7, 7), s_swap(q1, 1), line(c1, outward), s_swap(far_map, 4), s_swap(dt_rows, 4)
    )
    own = [stack(tokens, y0), a1]
    across = [stack(xp, xy), xa1]
    dt_rows = stack(dt_rows, dt_far)
    q2 = jnp.where(middle, c1, o1)
    a2 = stack(q1, yq1)
    maps = stack(own_map, far_map)
    half = main[6].shape[0] // 2
    q2, a2, maps, m5, m6, m1 = together(q2, a2, maps, main[5], main[6][:half], main[1])
    xa2, w6a, w5, yq2, maps_z, w1 = together(
        x_swap(a2), s_swap(m6, 6), s_swap(m5, 5), s_swap(q2, 1), s_swap(maps, 2), s_swap(m1, 1)
    )
    a3 = stack(q2, yq2)
    a3, maps, maps_z, m4, m6, m3, m2 = together(
        a3, maps, maps_z, main[4], main[6][half:], main[3], main[2]
    )
    maps = stack(maps, maps_z)
    xa3, w4, maps_y, w6b, w3, w2 = together(
        x_swap(a3), s_swap(m4, 4), s_swap(maps, 1), s_swap(m6, 6), s_swap(m3, 3), s_swap(m2, 2)
    )
    own += [a2, a3]
    across += [xa2]
    gathered = [both_cores(v) for v in own + across]
    last = (xa3, swap(xa3, "head", 1))
    mains = [main[0], w1, w2, w3, w4, w5, stack(w6a, w6b), w7]
    krows = far_map.shape[0]
    place = {0: (maps, 0), 4: (maps, 1), 2: (maps, 2), 6: (maps, 3)}
    place.update({d | 1: (maps_y, n) for d, (_, n) in list(place.items())})
    maps_of = [(0 if place[d][0] is maps else 1, place[d][1] * krows) for d in range(8)]
    return gathered, last, mains, (maps, maps_y), maps_of, dt_rows


def piece_table(shards):
    me = lax.axis_index("seq")
    shard = jnp.arange(shards)
    outer = (shard // 2) ^ (me // 2)
    middle = (me // 2 == 1) | (me // 2 == 2)
    slot = jnp.where((outer >= 2) & middle, outer ^ 1, outer)
    return slot * 2 + ((shard ^ me) & 1)


def head_split_body(
    tokens, norm_gain, w_in, w_dt, dt_bias, a_log, d_skip, conv_w, conv_b, gate_gain, w_out
):
    shards, blocks = lax.axis_size("seq"), lax.axis_size("head")
    s, h = lax.axis_index("seq"), lax.axis_index("head")
    rows = tokens.shape[0]
    krows, groups, wide = w_in.shape
    group_width = gate_gain.shape[1]
    state_size = (conv_b.shape[1] - group_width) // 2
    local_heads = dt_bias.shape[0]
    heads = local_heads // shards
    width = groups * group_width // local_heads
    chans = heads * width
    per = shards // groups
    dim = krows * shards

    gain = lax.dynamic_slice_in_dim(norm_gain, s * krows, krows, 0)

    def columns(t, first, count):
        part = lax.dynamic_slice(w_in, (0, t // per, first), (krows, 1, count))[:, 0]
        return (part.astype(jnp.float32) * gain[:, None]).astype(jnp.bfloat16)

    main = []
    for d in range(shards):
        t = s ^ d
        first = (t % per) * chans
        main.append(
            jnp.concatenate([columns(t, first, chans), columns(t, group_width + first, chans)], axis=1)
        )
    far_map = columns(s ^ per, 2 * group_width, 2 * state_size)
    own_map = columns(s, 2 * group_width, 2 * state_size)
    dt_rows = (w_dt.T.astype(jnp.float32) * gain[None, :]).astype(jnp.bfloat16)
    gathered, last, mains, maps, maps_of, dt_rows = exchange(tokens, main, far_map, own_map, dt_rows)
    dt_rows = lax.dynamic_slice_in_dim(dt_rows.reshape(shards, local_heads, krows), s * heads, heads, 1)
    dt_w = jnp.pad(jnp.swapaxes(dt_rows, 1, 2), ((0, 0), (0, 0), (0, LANES - heads)))

    group = s // per
    quarter = (s % per) * chans

    def own_channels(a):
        a = lax.dynamic_index_in_dim(a, group, a.ndim - 2, keepdims=False)
        inputs = lax.dynamic_slice_in_dim(a, quarter, chans, a.ndim - 1)
        return jnp.concatenate([inputs, a[..., group_width:]], axis=-1)

    def own_heads(a):
        return lax.dynamic_slice_in_dim(a, s * heads, heads, 0)

    def lanes(a):
        return jnp.pad(a, (0, LANES - heads))[None, :]

    where = jnp.concatenate([jnp.stack([s, h]), piece_table(shards)]).astype(jnp.int32)
    gated = mixer(
        where,
        gathered,
        last,
        mains,
        maps,
        maps_of,
        dt_w,
        own_channels(conv_w),
        own_channels(conv_b)[None, :],
        lanes(own_heads(dt_bias)),
        lanes(-jnp.exp(own_heads(a_log))),
        jnp.repeat(own_heads(d_skip), width)[None, :],
        rows,
        heads,
        width,
        dim,
    )
    blocks_out = [
        lax.dynamic_slice_in_dim(gated, (s ^ d) * rows, rows, 0) for d in range(shards)
    ]
    arrived = [blocks_out[0]] + [None] * (shards - 1)
    for d in range(shards - 1, 0, -1):
        arrived[d] = swap(blocks_out[d], "seq", d)

    gains = gate_gain.reshape(shards, chans)
    w_flat = w_out.reshape(groups * group_width, w_out.shape[2])
    wide = jnp.float32
    first, flat = out_terms(
        partial(normed_terms_kernel, (shards, chans, groups)), where, [*arrived, gains], w_flat, rows, blocks, 3, True
    )
    via_core = swap(first, "head", 1)
    second = out_terms(terms_kernel, where, [flat], w_flat, rows, blocks, 2, False)
    beyond = swap((second.astype(wide) + via_core.astype(wide)).astype(jnp.bfloat16), "head", 2)
    third = out_terms(terms_kernel, where, [flat], w_flat, rows, blocks, 1, False)
    from_core = swap(third, "head", 1)
    own = out_terms(terms_kernel, where, [flat], w_flat, rows, blocks, 0, False)
    return (own.astype(wide) + from_core.astype(wide) + beyond.astype(wide)).astype(jnp.bfloat16)


def fits_head_split(mesh, w_in, gate_gain, dt_bias):
    shards, blocks = mesh.shape["seq"], mesh.shape["head"]
    groups = gate_gain.shape[0] // blocks
    local_heads = dt_bias.shape[0] // blocks
    chans = groups * gate_gain.shape[1] // shards
    return shards == 8 and blocks == 4 and groups == 2 and local_heads % shards == 0 and chans % LANES == 0


def from_behind(shard, axis, by):
    count = lax.axis_size(axis)
    pairs = [(i, i + by) for i in range(count) if 0 <= i + by < count]
    return lax.ppermute(shard, axis, pairs)


def carried_in(shard, axis, combine, identity):
    count, index = (lax.axis_size(axis), lax.axis_index(axis))
    everything = jax.tree.map(
        lambda part, kind: lax.all_gather(part.astype(kind), axis),
        shard,
        (jnp.bfloat16, jnp.bfloat16),
    )
    start = jax.tree.map(
        lambda part, zero: jnp.broadcast_to(jnp.asarray(zero, part.dtype), part.shape),
        shard,
        identity,
    )

    def lap(k, before):
        reached = k < index
        new = combine(
            before, jax.tree.map(lambda part, own: part[k].astype(own.dtype), everything, shard)
        )
        return jax.tree.map(lambda a, b: jnp.where(reached, a, b), new, before)

    return lax.fori_loop(0, count, lap, start)


def normalize(values, gain):
    squares = jnp.mean(values * values, axis=-1, keepdims=True)
    return values * lax.rsqrt(squares + EPS) * gain


def state_block(inputs, step_size, log_decay, in_map, out_map, block_len):
    length = inputs.shape[0]
    stretch_count = length // block_len
    head_count = inputs.shape[1]
    head_size = inputs.shape[2]
    state_size = in_map.shape[1]
    shaped = (
        inputs.reshape(stretch_count, block_len, head_count, head_size),
        step_size.reshape(stretch_count, block_len, head_count),
        log_decay.reshape(stretch_count, block_len, head_count),
        in_map.reshape(stretch_count, block_len, state_size),
        out_map.reshape(stretch_count, block_len, state_size),
    )
    causal = jnp.arange(block_len)[:, None] >= jnp.arange(block_len)[None, :]

    def advance(state_now, pieces):
        stretch_in, stretch_step, stretch_log, stretch_b, stretch_c = pieces
        cumulative = jnp.cumsum(stretch_log, axis=0)
        gap_log = cumulative[:, None, :] - cumulative[None, :, :]
        decays = jnp.where(
            causal[:, :, None], jnp.exp(jnp.where(causal[:, :, None], gap_log, 0.0)), 0.0
        )
        scores = jnp.dot(stretch_c, stretch_b.T, preferred_element_type=jnp.float32)
        wide_c = stretch_c.astype(jnp.float32)
        wide_b = stretch_b.astype(jnp.float32)
        weights = scores[:, :, None] * decays * stretch_step[None, :, :]
        within = jnp.einsum("ijh,jhp->ihp", weights, stretch_in, precision=HIGHEST)
        across = jnp.exp(cumulative)[:, :, None] * jnp.einsum(
            "in,hpn->ihp", wide_c, state_now, precision=HIGHEST
        )
        to_end = jnp.exp(cumulative[-1][None, :] - cumulative) * stretch_step
        fresh_state = jnp.einsum("jh,jhp,jn->hpn", to_end, stretch_in, wide_b, precision=HIGHEST)
        state_next = jnp.exp(cumulative[-1])[:, None, None] * state_now + fresh_state
        return (state_next, within + across)

    start_state = jnp.zeros((head_count, head_size, state_size), jnp.float32)
    final, outputs = lax.scan(advance, start_state, shaped)
    return (outputs.reshape(length, head_count, head_size), final)


def link_states(earlier, later):
    return (earlier[0] + later[0], jnp.exp(later[0])[:, :, None, None] * earlier[1] + later[1])


def sequence_split_body(tokens, norm_gain, w_in, w_dt, dt_bias, a_log, d_skip, conv_w, conv_b, gate_gain, w_out):
    local_rows = tokens.shape[0]
    kernel_len = conv_w.shape[0]
    groups, group_width = gate_gain.shape
    head_count = dt_bias.shape[0]
    per_group = head_count // groups
    head_size = group_width // per_group
    state_size = (conv_b.shape[1] - group_width) // 2
    gathered = lax.all_gather(tokens, "head", axis=1, tiled=True)
    normed = normalize(gathered.astype(jnp.float32), norm_gain).astype(jnp.bfloat16)
    span_rows = normed.shape[0]
    flat_in = w_in.reshape(w_in.shape[0], groups * w_in.shape[2])
    proj_sum = jnp.dot(
        normed,
        lax.all_gather(flat_in, "seq", axis=0, tiled=True),
        preferred_element_type=jnp.float32,
    )
    step_sum = jnp.dot(
        normed, lax.all_gather(w_dt, "seq", axis=0, tiled=True), preferred_element_type=jnp.float32
    )
    projected = proj_sum.astype(jnp.bfloat16).reshape(span_rows, groups, w_in.shape[2])
    step_size = jax.nn.softplus(step_sum + dt_bias[None, :])
    gate_raw = projected[span_rows - local_rows :, :, :group_width]
    own_channels = projected[:, :, group_width:]
    rim_rows = from_behind(own_channels[local_rows - kernel_len + 1 :], "seq", 1)
    extended = jnp.concatenate([rim_rows, own_channels], axis=0)
    summed = conv_b[None, :, :]
    for offset in range(kernel_len):
        summed = summed + conv_w[offset][None, :, :] * extended[
            offset : offset + local_rows
        ].astype(jnp.float32)
    narrow = lax.optimization_barrier(jax.nn.silu(summed).astype(jnp.bfloat16))
    convolved = narrow.astype(jnp.float32)
    inputs = convolved[:, :, :group_width].reshape(local_rows, groups, per_group, head_size)
    in_map = narrow[:, :, group_width : group_width + state_size]
    out_map = narrow[:, :, group_width + state_size :]
    step_grouped = step_size.reshape(local_rows, groups, per_group)
    log_decay = -jnp.exp(a_log).reshape(groups, per_group)[None, :, :] * step_grouped
    run_block = jax.vmap(
        partial(state_block, block_len=STRETCH), in_axes=(1, 1, 1, 1, 1), out_axes=(1, 0)
    )
    local_out, ending = run_block(inputs, step_grouped, log_decay, in_map, out_map)
    totals = jnp.sum(log_decay, axis=0)
    identity = (jnp.zeros_like(totals), jnp.zeros_like(ending))
    prior_decay, incoming = carried_in((totals, ending), "seq", link_states, identity)
    cumulative = jnp.exp(jnp.cumsum(log_decay, axis=0))
    carried = (
        jnp.einsum("tgn,ghpn->tghp", out_map.astype(jnp.float32), incoming, precision=HIGHEST)
        * cumulative[:, :, :, None]
    )
    outputs = local_out + carried + d_skip.reshape(groups, per_group)[None, :, :, None] * inputs
    gated = outputs.reshape(local_rows, groups, group_width) * jax.nn.silu(
        gate_raw.astype(jnp.float32)
    )
    normed_out = normalize(gated, gate_gain[None, :, :]).astype(jnp.bfloat16)
    flat_out = normed_out.reshape(local_rows, groups * group_width)
    terms = jnp.dot(
        flat_out,
        w_out.reshape(groups * group_width, w_out.shape[2]),
        preferred_element_type=jnp.float32,
    )
    return lax.psum_scatter(terms.astype(jnp.bfloat16), "head", scatter_dimension=1, tiled=True)


def solution(mesh):
    in_specs = (
        P("seq", "head"),
        P(),
        P("seq", "head", None),
        P("seq", "head"),
        P("head"),
        P("head"),
        P("head"),
        P(None, "head", None),
        P("head", None),
        P("head", None),
        P("head", None, None),
    )
    out_specs = P("seq", "head")

    def mixer_prefill(*args):
        by_heads = fits_head_split(mesh, args[2], args[9], args[4])
        body = head_split_body if by_heads else sequence_split_body
        mapped = jax.shard_map(
            body, mesh=mesh, in_specs=in_specs, out_specs=out_specs, check_vma=False
        )
        return mapped(*args)

    return mixer_prefill
```

```python
from functools import partial

import jax
import jax.numpy as jnp
from jax import lax
from jax.experimental import pallas as pl
from jax.experimental.pallas import tpu as pltpu
from jax.sharding import PartitionSpec as P

STRETCH = 128


EPS = 1e-05
HIGHEST = lax.Precision.HIGHEST
VMEM_LIMIT = 58 * 1024 * 1024
LANES = 128


def swap(value, axis, bit):
    count = lax.axis_size(axis)
    return lax.ppermute(value, axis, [(i, i ^ bit) for i in range(count)])


def silu_of(v):
    half = 0.5 * v
    return half + half * jnp.tanh(half)


def mixer_kernel(
    cfg,
    where_ref,
    *refs,
):
    (shards, maps_of, parts, dt_rows, blocks, rows, feats, krows, heads, width, state_size, taps, dim) = cfg
    many = shards - 1
    gathered, last = refs[:many], refs[many : many + 2]
    at = many + 2
    mains = []
    for n in parts:
        mains.append(refs[at : at + n])
        at += n
    (map_a, map_b, conv_w, conv_b, dt_bias, neg_rate, skip) = refs[at : at + 7]
    (out_ref, wbuf, dt_all, dt_own, xbuf, pbuf, pnext, cbuf, state, wsem, dsem, xsem) = refs[at + 7 :]
    i = pl.program_id(0)
    steps = pl.num_programs(0)
    me_s, me_h = where_ref[0], where_ref[1]
    chans = heads * width
    conv_cols = chans + 2 * state_size
    main_cols = 2 * chans
    map_cols = 2 * state_size
    per = feats // krows
    map_rows = krows + dt_rows * (krows // (2 * state_size))
    me_q = me_s % (shards // 2)

    def move(copy, start):
        if start:
            copy.start()
        else:
            copy.wait()

    def fetch(step, slot, start):
        which = where_ref[2 + step]
        for k in range(shards // 2):
            for inner in (0, 1):
                @pl.when(which == 2 * k + inner)
                def _(k=k, inner=inner):
                    part = pl.ds(inner * rows, rows)
                    for e in range(blocks):
                        beyond, core = divmod(e, 2)
                        array = k + beyond * (shards // 2)
                        if array < many:
                            src, block = gathered[array].at[core, part, :], e
                        else:
                            src, block = last[core].at[part, :], (e & ~1) + ((me_h & 1) ^ core)
                        dst = xbuf.at[slot, :, pl.ds(pl.multiple_of(block * feats, feats), feats)]
                        move(pltpu.make_async_copy(src, dst, xsem.at[slot, e]), start)

    def weights(start):
        for d in range(shards):
            kb = me_s ^ d
            block = kb // per
            place = ((block // 2) ^ (me_h // 2)) * 2 + (block % 2)
            row = pl.multiple_of(place * feats + (kb % per) * krows, krows)
            source, place_row = maps_of[d]
            map_src = (map_a, map_b)[source]
            lo_row = place_row * map_rows
            depth = krows // len(mains[d])
            for n, src in enumerate(mains[d]):
                dst = wbuf.at[pl.ds(row + n * depth, depth), pl.ds(0, main_cols)]
                move(pltpu.make_async_copy(src, dst, wsem.at[n, d]), start)
            dst = wbuf.at[pl.ds(row, krows), pl.ds(main_cols, map_cols)]
            move(pltpu.make_async_copy(map_src.at[pl.ds(lo_row, krows), :], dst, wsem.at[2, d]), start)
            for n in range(krows // map_cols):
                src = map_src.at[pl.ds(lo_row + krows + n * dt_rows, dt_rows), :]
                dst = dt_all.at[:, pl.ds(pl.multiple_of(row + n * map_cols, map_cols), map_cols)]
                move(pltpu.make_async_copy(src, dst, dsem.at[n, d]), start)

    slot = lax.rem(i, 2)
    shard_count = steps - 1

    @pl.when(i == 0)
    def _():
        fetch(0, 0, True)
        weights(True)
        state[...] = jnp.zeros_like(state)
        cbuf[0:8, :] = jnp.zeros((8, conv_cols), jnp.float32)

    @pl.when(i + 1 < shard_count)
    def _():
        fetch(i + 1, 1 - slot, True)

    @pl.when(i == 0)
    def _():
        weights(False)
        own_row = lax.broadcasted_iota(jnp.int32, (LANES, dt_rows), 0)
        group_row = lax.broadcasted_iota(jnp.int32, (LANES, dt_rows), 1)
        mine = (group_row == own_row + me_q * heads) & (own_row < heads)
        pick = jnp.where(mine, 1.0, 0.0).astype(jnp.bfloat16)
        for lo in range(0, dim, feats):
            dt_own[:, lo : lo + feats] = jnp.dot(
                pick, dt_all[:, lo : lo + feats], preferred_element_type=jnp.float32
            ).astype(jnp.bfloat16)

    @pl.when(i < shard_count)
    def _():
        fetch(i, slot, False)

    total = main_cols + map_cols + LANES
    tiles = [(lo, min(256, total - lo)) for lo in range(0, total, 256)]
    length = STRETCH
    stretches = rows // length

    def row_factor():
        squares = jnp.zeros((rows, 1), jnp.float32)
        for e in range(blocks):
            part = xbuf[slot, :, e * feats : (e + 1) * feats].astype(jnp.float32)
            squares = squares + jnp.sum(part * part, axis=1, keepdims=True)
        return lax.rsqrt(squares * (1.0 / dim) + EPS)

    def project(tile, factor):
        lo, cols = tile
        if lo < total - LANES:
            part = jnp.dot(xbuf[slot], wbuf[:, lo : lo + cols], preferred_element_type=jnp.float32)
        else:
            part = lax.dot_general(
                xbuf[slot], dt_own[...], (((1,), (1,)), ((), ())), preferred_element_type=jnp.float32
            )
        pnext[:, lo : lo + cols] = part * factor

    def hand_over():
        pbuf[:, :chans] = pnext[:, :chans]
        pbuf[:, chans:] = pnext[:, total - LANES :]
        cbuf[8 : 8 + rows, :] = pnext[:, chans : chans + conv_cols]

    def constants():
        tri = lax.broadcasted_iota(jnp.int32, (length, length), 0) >= lax.broadcasted_iota(
            jnp.int32, (length, length), 1
        )
        ones = jnp.where(tri, 1.0, 0.0).astype(jnp.float32)
        row = lax.broadcasted_iota(jnp.int32, (2 * LANES, chans), 0) % LANES
        lane = lax.broadcasted_iota(jnp.int32, (2 * LANES, chans), 1) // width
        widen = jnp.where(row == lane, 1.0, 0.0).astype(jnp.bfloat16)
        lane_head = lax.broadcasted_iota(jnp.int32, (1, chans), 1) // width
        masks = [jnp.where(lane_head == j, 1.0, 0.0).astype(jnp.bfloat16) for j in range(heads)]
        return tri, ones, widen, masks

    def scan(st, tri, ones, widen, masks):
        r0 = st * length
        summed = conv_b[...]
        for k in range(taps):
            first = 8 - (taps - 1) + k + r0
            summed = summed + conv_w[k : k + 1, :] * cbuf[first : first + length, :]
        narrow = silu_of(summed).astype(jnp.bfloat16)
        in_map = narrow[:, chans : chans + state_size]
        out_map = narrow[:, chans + state_size :]
        xf = narrow[:, :chans].astype(jnp.float32)
        raw = pbuf[r0 : r0 + length, chans:] + dt_bias[...]
        step = jnp.maximum(raw, 0.0) + jnp.log1p(jnp.exp(-jnp.abs(raw)))
        logd = neg_rate[...] * step
        cum = jnp.dot(ones, logd, preferred_element_type=jnp.float32, precision=HIGHEST)
        cum_t = cum.T
        columns = jnp.concatenate([jnp.exp(cum), step, jnp.exp(cum[length - 1 :, :] - cum)], axis=0)
        high = columns.astype(jnp.bfloat16)
        low = (columns - high.astype(jnp.float32)).astype(jnp.bfloat16)
        wide = jnp.dot(jnp.concatenate([high, low], axis=1), widen, preferred_element_type=jnp.float32)
        since, stepped, to_end = wide[:length], wide[length : 2 * length], wide[2 * length :]
        scores = lax.dot_general(
            out_map, in_map, (((1,), (1,)), ((), ())), preferred_element_type=jnp.float32
        )
        scores = jnp.where(tri, scores, 0.0)
        taken = xf * stepped
        taken_low = taken.astype(jnp.bfloat16)
        weighted, spaced = [], []
        for j in range(heads):
            gap = jnp.minimum(cum[:, j : j + 1] - cum_t[j : j + 1, :], 0.0)
            weighted.append((scores * jnp.exp(gap)).astype(jnp.bfloat16))
            spaced.append(taken_low * masks[j])
        within = jnp.dot(
            jnp.concatenate(weighted, axis=1),
            jnp.concatenate(spaced, axis=0),
            preferred_element_type=jnp.float32,
        )
        now = state[...]
        across = jnp.dot(out_map, now.astype(jnp.bfloat16), preferred_element_type=jnp.float32)
        y = within + since * across + skip[...] * xf
        fresh = lax.dot_general(
            in_map, (taken * to_end).astype(jnp.bfloat16), (((0,), (0,)), ((), ())), preferred_element_type=jnp.float32
        )
        state[...] = since[length - 1 :, :] * now + fresh
        gate = pbuf[r0 : r0 + length, :chans]
        out_ref[r0 : r0 + length, :] = (y * silu_of(gate)).astype(jnp.bfloat16)

    def keep_tail():
        cbuf[0:8, :] = cbuf[rows : rows + 8, :]

    @pl.when(i == 0)
    def _():
        factor = row_factor()
        for tile in tiles:
            project(tile, factor)
        hand_over()

    @pl.when((i > 0) & (i < shard_count))
    def _():
        held = constants()
        factor = row_factor()
        for n in range(max(len(tiles), stretches)):
            if n < len(tiles):
                project(tiles[n], factor)
            if n < stretches:
                scan(n, *held)
        keep_tail()
        hand_over()

    @pl.when(i == shard_count)
    def _():
        held = constants()
        for n in range(stretches):
            scan(n, *held)


def mixer(
    where, gathered, last, mains, maps, maps_of, conv_w, conv_b, dt_bias, neg_rate, skip, rows, heads, width, dim
):
    shards = len(mains)
    feats = last[0].shape[1]
    blocks = dim // feats
    krows = mains[0].shape[0]
    chans = heads * width
    state_size = maps[0].shape[1] // 2
    parts = tuple(len(m) if isinstance(m, tuple) else 1 for m in mains)
    dt_rows = heads * shards // 2
    taps = conv_w.shape[0]
    total = 2 * chans + 2 * state_size + LANES
    cfg = (shards, tuple(maps_of), parts, dt_rows, blocks, rows, feats, krows, heads, width, state_size, taps, dim)
    hbm = pl.BlockSpec(memory_space=pl.ANY)

    def whole(a):
        return pl.BlockSpec(a.shape, lambda i, w: (0,) * a.ndim)

    small = (conv_w, conv_b, dt_bias, neg_rate, skip)
    flat_mains = [part for m in mains for part in (m if isinstance(m, tuple) else (m,))]
    large = (*gathered, *last, *flat_mains, *maps)
    return pl.pallas_call(
        partial(mixer_kernel, cfg),
        out_shape=jax.ShapeDtypeStruct((rows * shards, chans), jnp.bfloat16),
        grid_spec=pltpu.PrefetchScalarGridSpec(
            num_scalar_prefetch=1,
            grid=(shards + 1,),
            in_specs=[hbm] * len(large) + [whole(a) for a in small],
            out_specs=pl.BlockSpec((rows, chans), lambda i, w: (jnp.maximum(i - 1, 0), 0)),
            scratch_shapes=[
                pltpu.VMEM((dim, total - LANES), jnp.bfloat16),
                pltpu.VMEM((dt_rows, dim), jnp.bfloat16),
                pltpu.VMEM((LANES, dim), jnp.bfloat16),
                pltpu.VMEM((2, rows, dim), jnp.bfloat16),
                pltpu.VMEM((rows, chans + LANES), jnp.float32),
                pltpu.VMEM((rows, total), jnp.float32),
                pltpu.VMEM((8 + rows, chans + 2 * state_size), jnp.float32),
                pltpu.VMEM((state_size, chans), jnp.float32),
                pltpu.SemaphoreType.DMA((3, shards)),
                pltpu.SemaphoreType.DMA((krows // (2 * state_size), shards)),
                pltpu.SemaphoreType.DMA((2, blocks)),
            ],
        ),
        compiler_params=pltpu.CompilerParams(vmem_limit_bytes=VMEM_LIMIT, dimension_semantics=("arbitrary",)),
        cost_estimate=pl.CostEstimate(
            flops=2 * rows * shards * dim * total, bytes_accessed=2 * rows * shards * dim, transcendentals=0
        ),
    )(where, *large, *small)


def terms_kernel(cfg, where_ref, *refs):
    shards, chans, groups, order, keep = cfg
    count = shards + 1 if keep else 1
    values, w_hbm, outs = refs[:count], refs[count], refs[count + 1 : count + 1 + len(order)]
    w_buf, sem = refs[-2], refs[-1]
    flat = refs[count + 1 + len(order)] if keep else values[0]
    depth, feats = w_buf.shape[1:]
    chunks = sem.shape[1]
    part_rows = depth // chunks
    me_s = where_ref[0]

    def copy(block, n):
        part = pl.ds(n * part_rows, part_rows)
        lane = pl.multiple_of((where_ref[1] ^ order[block]) * feats, feats)
        return pltpu.make_async_copy(
            w_hbm.at[part, pl.ds(lane, feats)], w_buf.at[block, part, :], sem.at[block, n]
        )

    for block in range(len(order)):
        for n in range(chunks):
            copy(block, n).start()
    if keep:
        gated, gain = values[:shards], values[shards]
        per = shards // groups
        for g in range(groups):
            squares = 0.0
            parts = []
            for d in range(g * per, (g + 1) * per):
                part = gated[d][...].astype(jnp.float32)
                parts.append(part)
                squares = squares + jnp.sum(part * part, axis=1, keepdims=True)
            factor = lax.rsqrt(squares * (1.0 / (per * chans)) + EPS)
            for d, part in zip(range(g * per, (g + 1) * per), parts):
                t = me_s ^ d
                value = (part * factor * gain[pl.ds(t, 1), :]).astype(jnp.bfloat16)
                flat[:, pl.ds(pl.multiple_of(t * chans, chans), chans)] = value
    for block, out_ref in enumerate(outs):
        for n in range(chunks):
            copy(block, n).wait()
        for lo in range(0, feats, 256):
            cols = min(256, feats - lo)
            out_ref[:, lo : lo + cols] = jnp.dot(
                flat[...], w_buf[block, :, lo : lo + cols], preferred_element_type=jnp.float32
            ).astype(jnp.bfloat16)


def out_terms(where, values, w_flat, shape, order, keep):
    shards, groups, rows, chans, blocks = shape
    depth, dim = w_flat.shape
    feats = dim // blocks
    vmem = pl.BlockSpec(memory_space=pltpu.VMEM)
    widths = [feats] * len(order) + ([depth] if keep else [])
    out_shape = tuple(jax.ShapeDtypeStruct((rows, n), jnp.bfloat16) for n in widths)
    return pl.pallas_call(
        partial(terms_kernel, (shards, chans, groups, order, keep)),
        out_shape=out_shape,
        in_specs=[pl.BlockSpec(memory_space=pltpu.SMEM)] + [vmem] * len(values) + [pl.BlockSpec(memory_space=pl.ANY)],
        out_specs=(vmem,) * len(widths),
        scratch_shapes=[
            pltpu.VMEM((len(order), depth, feats), jnp.bfloat16),
            pltpu.SemaphoreType.DMA((len(order), 8)),
        ],
        compiler_params=pltpu.CompilerParams(vmem_limit_bytes=VMEM_LIMIT),
        cost_estimate=pl.CostEstimate(
            flops=rows * feats,
            bytes_accessed=rows * feats,
            transcendentals=0,
        ),
    )(where, *values, w_flat)


def line(value, pairs):
    return lax.ppermute(value, "seq", [(2 * a + y, 2 * b + y) for a, b in pairs for y in (0, 1)])


def stack(*parts):
    return jnp.concatenate(parts, axis=0)


def both_cores(value):
    pairs = [[i, i + 1] for i in range(0, lax.axis_size("head"), 2)]
    return lax.all_gather(value, "head", axis=0, axis_index_groups=pairs)


def together(*values):
    return lax.optimization_barrier(values)


def exchange(tokens, w_in, weights_of):
    at = lax.axis_index("seq") // 2
    middle = (at == 1) | (at == 2)
    cross, outward = [(1, 2), (2, 1)], [(1, 0), (2, 3)]

    def x_swap(v):
        return swap(v, "head", 2)

    def s_swap(v, bit):
        return swap(v, "seq", bit)

    xp, y0, z1, c0, (m1, m7, far_map), w_in = together(
        x_swap(tokens),
        s_swap(tokens, 1),
        s_swap(tokens, 2),
        line(tokens, cross),
        weights_of(w_in, (1, 7, "far")),
        w_in,
    )
    xy, yz1, c1, o0, (m2, m6, m5, m4, m3, m0, own_map) = together(
        x_swap(y0),
        s_swap(z1, 1),
        line(z1, cross),
        line(c0, outward),
        weights_of(w_in, (2, 6, 5, 4, 3, 0, "own")),
    )
    q1 = jnp.where(middle, c0, o0)
    q1, z1, yz1, c1, m7, far_map = together(q1, z1, yz1, c1, m7, far_map)
    a1 = stack(z1, yz1)
    xa1, w7, yq1, o1, far_map = together(
        x_swap(a1), s_swap(m7, 7), s_swap(q1, 1), line(c1, outward), s_swap(far_map, 4)
    )
    own = [stack(tokens, y0), a1]
    across = [stack(xp, xy), xa1]
    q2 = jnp.where(middle, c1, o1)
    a2 = stack(q1, yq1)
    maps = stack(own_map, far_map)
    half = m6.shape[0] // 2
    q2, a2, maps, m5, m6a, m6b = together(q2, a2, maps, m5, m6[:half], m6[half:])
    xa2, w5, w6a, yq2, maps_z = together(
        x_swap(a2), s_swap(m5, 5), s_swap(m6a, 6), s_swap(q2, 1), s_swap(maps, 2)
    )
    a3 = stack(q2, yq2)
    maps = stack(maps, maps_z)
    a3, maps, m4, m6b, m3 = together(a3, maps, m4, m6b, m3)
    xa3, w4, w6b, maps_y, w3 = together(
        x_swap(a3), s_swap(m4, 4), s_swap(m6b, 6), s_swap(maps, 1), s_swap(m3, 3)
    )
    own += [a2, a3]
    across += [xa2]
    gathered = [both_cores(v) for v in own + across]
    m1, m2, xa3, w3 = together(m1, m2, xa3, w3)
    w1, w2 = s_swap(m1, 1), s_swap(m2, 2)
    last = (xa3, swap(xa3, "head", 1))
    mains = [m0, w1, w2, w3, w4, w5, (w6a, w6b), w7]
    place = {0: 0, 4: 1, 2: 2, 6: 3}
    maps_of = [(d & 1, place[d & ~1]) for d in range(8)]
    return gathered, last, mains, (maps, maps_y), maps_of


def piece_table(shards):
    me = lax.axis_index("seq")
    shard = jnp.arange(shards)
    outer = (shard // 2) ^ (me // 2)
    middle = (me // 2 == 1) | (me // 2 == 2)
    slot = jnp.where((outer >= 2) & middle, outer ^ 1, outer)
    return slot * 2 + ((shard ^ me) & 1)


def head_split_body(
    tokens, norm_gain, w_in, w_dt, dt_bias, a_log, d_skip, conv_w, conv_b, gate_gain, w_out
):
    shards, blocks = lax.axis_size("seq"), lax.axis_size("head")
    s, h = lax.axis_index("seq"), lax.axis_index("head")
    rows = tokens.shape[0]
    krows, groups, wide = w_in.shape
    group_width = gate_gain.shape[1]
    state_size = (conv_b.shape[1] - group_width) // 2
    local_heads = dt_bias.shape[0]
    heads = local_heads // shards
    width = groups * group_width // local_heads
    chans = heads * width
    per = shards // groups
    dim = krows * shards

    gain = lax.dynamic_slice_in_dim(norm_gain, s * krows, krows, 0)

    dt_cols = local_heads // groups

    def weights_of(w_in, names):
        def columns(t, first, count):
            part = lax.dynamic_slice(w_in, (0, t // per, first), (krows, 1, count))[:, 0]
            return (part.astype(jnp.float32) * gain[:, None]).astype(jnp.bfloat16)

        def one(name):
            if name in ("far", "own"):
                t = s ^ per if name == "far" else s
                dt = lax.dynamic_slice_in_dim(w_dt, (t // per) * dt_cols, dt_cols, 1).T
                dt = (dt.astype(jnp.float32) * gain[None, :]).astype(jnp.bfloat16)
                cols = 2 * state_size
                rows_of_dt = [dt[:, lo : lo + cols] for lo in range(0, krows, cols)]
                return jnp.concatenate([columns(t, 2 * group_width, cols), *rows_of_dt], axis=0)
            t = s ^ name
            first = (t % per) * chans
            return jnp.concatenate(
                [columns(t, first, chans), columns(t, group_width + first, chans)], axis=1
            )

        return tuple(one(name) for name in names)

    gathered, last, mains, maps, maps_of = exchange(tokens, w_in, weights_of)

    group = s // per
    quarter = (s % per) * chans

    def own_channels(a):
        a = lax.dynamic_index_in_dim(a, group, a.ndim - 2, keepdims=False)
        inputs = lax.dynamic_slice_in_dim(a, quarter, chans, a.ndim - 1)
        return jnp.concatenate([inputs, a[..., group_width:]], axis=-1)

    def own_heads(a):
        return lax.dynamic_slice_in_dim(a, s * heads, heads, 0)

    def lanes(a):
        return jnp.pad(a, (0, LANES - heads))[None, :]

    where = jnp.concatenate([jnp.stack([s, h]), piece_table(shards)]).astype(jnp.int32)
    gated = mixer(
        where,
        gathered,
        last,
        mains,
        maps,
        maps_of,
        own_channels(conv_w),
        own_channels(conv_b)[None, :],
        lanes(own_heads(dt_bias)),
        lanes(-jnp.exp(own_heads(a_log))),
        jnp.repeat(own_heads(d_skip), width)[None, :],
        rows,
        heads,
        width,
        dim,
    )
    blocks_out = [
        lax.dynamic_slice_in_dim(gated, (s ^ d) * rows, rows, 0) for d in range(shards)
    ]
    arrived = [blocks_out[0]] + [None] * (shards - 1)
    for d in range(shards - 1, 0, -1):
        arrived[d] = swap(blocks_out[d], "seq", d)

    gains = gate_gain.reshape(shards, chans)
    w_flat = w_out.reshape(groups * group_width, w_out.shape[2])
    wide = jnp.float32
    shape = (shards, groups, rows, chans, blocks)
    shape = (shards, groups, rows, chans, blocks)
    first, flat = out_terms(where, [*arrived, gains], w_flat, shape, (3,), True)
    via_core = swap(first, "head", 1)
    (second,) = out_terms(where, [flat], w_flat, shape, (2,), False)
    to_pair, flat = together((second.astype(wide) + via_core.astype(wide)).astype(jnp.bfloat16), flat)
    beyond = swap(to_pair, "head", 2)
    third, own = out_terms(where, [flat], w_flat, shape, (1, 0), False)
    from_core = swap(third, "head", 1)
    return (own.astype(wide) + from_core.astype(wide) + beyond.astype(wide)).astype(jnp.bfloat16)


def fits_head_split(mesh, w_in, gate_gain, dt_bias):
    shards, blocks = mesh.shape["seq"], mesh.shape["head"]
    groups = gate_gain.shape[0] // blocks
    local_heads = dt_bias.shape[0] // blocks
    chans = groups * gate_gain.shape[1] // shards
    return shards == 8 and blocks == 4 and groups == 2 and local_heads % shards == 0 and chans % LANES == 0


def from_behind(shard, axis, by):
    count = lax.axis_size(axis)
    pairs = [(i, i + by) for i in range(count) if 0 <= i + by < count]
    return lax.ppermute(shard, axis, pairs)


def carried_in(shard, axis, combine, identity):
    count, index = (lax.axis_size(axis), lax.axis_index(axis))
    everything = jax.tree.map(
        lambda part, kind: lax.all_gather(part.astype(kind), axis),
        shard,
        (jnp.bfloat16, jnp.bfloat16),
    )
    start = jax.tree.map(
        lambda part, zero: jnp.broadcast_to(jnp.asarray(zero, part.dtype), part.shape),
        shard,
        identity,
    )

    def lap(k, before):
        reached = k < index
        new = combine(
            before, jax.tree.map(lambda part, own: part[k].astype(own.dtype), everything, shard)
        )
        return jax.tree.map(lambda a, b: jnp.where(reached, a, b), new, before)

    return lax.fori_loop(0, count, lap, start)


def normalize(values, gain):
    squares = jnp.mean(values * values, axis=-1, keepdims=True)
    return values * lax.rsqrt(squares + EPS) * gain


def state_block(inputs, step_size, log_decay, in_map, out_map, block_len):
    length = inputs.shape[0]
    stretch_count = length // block_len
    head_count = inputs.shape[1]
    head_size = inputs.shape[2]
    state_size = in_map.shape[1]
    shaped = (
        inputs.reshape(stretch_count, block_len, head_count, head_size),
        step_size.reshape(stretch_count, block_len, head_count),
        log_decay.reshape(stretch_count, block_len, head_count),
        in_map.reshape(stretch_count, block_len, state_size),
        out_map.reshape(stretch_count, block_len, state_size),
    )
    causal = jnp.arange(block_len)[:, None] >= jnp.arange(block_len)[None, :]

    def advance(state_now, pieces):
        stretch_in, stretch_step, stretch_log, stretch_b, stretch_c = pieces
        cumulative = jnp.cumsum(stretch_log, axis=0)
        gap_log = cumulative[:, None, :] - cumulative[None, :, :]
        decays = jnp.where(
            causal[:, :, None], jnp.exp(jnp.where(causal[:, :, None], gap_log, 0.0)), 0.0
        )
        scores = jnp.dot(stretch_c, stretch_b.T, preferred_element_type=jnp.float32)
        wide_c = stretch_c.astype(jnp.float32)
        wide_b = stretch_b.astype(jnp.float32)
        weights = scores[:, :, None] * decays * stretch_step[None, :, :]
        within = jnp.einsum("ijh,jhp->ihp", weights, stretch_in, precision=HIGHEST)
        across = jnp.exp(cumulative)[:, :, None] * jnp.einsum(
            "in,hpn->ihp", wide_c, state_now, precision=HIGHEST
        )
        to_end = jnp.exp(cumulative[-1][None, :] - cumulative) * stretch_step
        fresh_state = jnp.einsum("jh,jhp,jn->hpn", to_end, stretch_in, wide_b, precision=HIGHEST)
        state_next = jnp.exp(cumulative[-1])[:, None, None] * state_now + fresh_state
        return (state_next, within + across)

    start_state = jnp.zeros((head_count, head_size, state_size), jnp.float32)
    final, outputs = lax.scan(advance, start_state, shaped)
    return (outputs.reshape(length, head_count, head_size), final)


def link_states(earlier, later):
    return (earlier[0] + later[0], jnp.exp(later[0])[:, :, None, None] * earlier[1] + later[1])


def sequence_split_body(tokens, norm_gain, w_in, w_dt, dt_bias, a_log, d_skip, conv_w, conv_b, gate_gain, w_out):
    local_rows = tokens.shape[0]
    kernel_len = conv_w.shape[0]
    groups, group_width = gate_gain.shape
    head_count = dt_bias.shape[0]
    per_group = head_count // groups
    head_size = group_width // per_group
    state_size = (conv_b.shape[1] - group_width) // 2
    gathered = lax.all_gather(tokens, "head", axis=1, tiled=True)
    normed = normalize(gathered.astype(jnp.float32), norm_gain).astype(jnp.bfloat16)
    span_rows = normed.shape[0]
    flat_in = w_in.reshape(w_in.shape[0], groups * w_in.shape[2])
    proj_sum = jnp.dot(
        normed,
        lax.all_gather(flat_in, "seq", axis=0, tiled=True),
        preferred_element_type=jnp.float32,
    )
    step_sum = jnp.dot(
        normed, lax.all_gather(w_dt, "seq", axis=0, tiled=True), preferred_element_type=jnp.float32
    )
    projected = proj_sum.astype(jnp.bfloat16).reshape(span_rows, groups, w_in.shape[2])
    step_size = jax.nn.softplus(step_sum + dt_bias[None, :])
    gate_raw = projected[span_rows - local_rows :, :, :group_width]
    own_channels = projected[:, :, group_width:]
    rim_rows = from_behind(own_channels[local_rows - kernel_len + 1 :], "seq", 1)
    extended = jnp.concatenate([rim_rows, own_channels], axis=0)
    summed = conv_b[None, :, :]
    for offset in range(kernel_len):
        summed = summed + conv_w[offset][None, :, :] * extended[
            offset : offset + local_rows
        ].astype(jnp.float32)
    narrow = lax.optimization_barrier(jax.nn.silu(summed).astype(jnp.bfloat16))
    convolved = narrow.astype(jnp.float32)
    inputs = convolved[:, :, :group_width].reshape(local_rows, groups, per_group, head_size)
    in_map = narrow[:, :, group_width : group_width + state_size]
    out_map = narrow[:, :, group_width + state_size :]
    step_grouped = step_size.reshape(local_rows, groups, per_group)
    log_decay = -jnp.exp(a_log).reshape(groups, per_group)[None, :, :] * step_grouped
    run_block = jax.vmap(
        partial(state_block, block_len=STRETCH), in_axes=(1, 1, 1, 1, 1), out_axes=(1, 0)
    )
    local_out, ending = run_block(inputs, step_grouped, log_decay, in_map, out_map)
    totals = jnp.sum(log_decay, axis=0)
    identity = (jnp.zeros_like(totals), jnp.zeros_like(ending))
    prior_decay, incoming = carried_in((totals, ending), "seq", link_states, identity)
    cumulative = jnp.exp(jnp.cumsum(log_decay, axis=0))
    carried = (
        jnp.einsum("tgn,ghpn->tghp", out_map.astype(jnp.float32), incoming, precision=HIGHEST)
        * cumulative[:, :, :, None]
    )
    outputs = local_out + carried + d_skip.reshape(groups, per_group)[None, :, :, None] * inputs
    gated = outputs.reshape(local_rows, groups, group_width) * jax.nn.silu(
        gate_raw.astype(jnp.float32)
    )
    normed_out = normalize(gated, gate_gain[None, :, :]).astype(jnp.bfloat16)
    flat_out = normed_out.reshape(local_rows, groups * group_width)
    terms = jnp.dot(
        flat_out,
        w_out.reshape(groups * group_width, w_out.shape[2]),
        preferred_element_type=jnp.float32,
    )
    return lax.psum_scatter(terms.astype(jnp.bfloat16), "head", scatter_dimension=1, tiled=True)


def solution(mesh):
    in_specs = (
        P("seq", "head"),
        P(),
        P("seq", "head", None),
        P("seq", "head"),
        P("head"),
        P("head"),
        P("head"),
        P(None, "head", None),
        P("head", None),
        P("head", None),
        P("head", None, None),
    )
    out_specs = P("seq", "head")

    def mixer_prefill(*args):
        by_heads = fits_head_split(mesh, args[2], args[9], args[4])
        body = head_split_body if by_heads else sequence_split_body
        mapped = jax.shard_map(
            body, mesh=mesh, in_specs=in_specs, out_specs=out_specs, check_vma=False
        )
        return mapped(*args)

    return mixer_prefill
```

```python
from functools import partial

import jax
import jax.numpy as jnp
from jax import lax
from jax.experimental import pallas as pl
from jax.experimental.pallas import tpu as pltpu
from jax.sharding import PartitionSpec as P

STRETCH = 128


EPS = 1e-05
HIGHEST = lax.Precision.HIGHEST
VMEM_LIMIT = 58 * 1024 * 1024
LANES = 128


def swap(value, axis, bit):
    count = lax.axis_size(axis)
    return lax.ppermute(value, axis, [(i, i ^ bit) for i in range(count)])


def silu_of(v):
    half = 0.5 * v
    return half + half * jnp.tanh(half)


def mixer_kernel(
    cfg,
    where_ref,
    *refs,
):
    (shards, maps_of, parts, dt_rows, blocks, rows, feats, krows, heads, width, state_size, taps, dim) = cfg
    many = shards - 1
    gathered, last = refs[:many], refs[many : many + 2]
    at = many + 2
    mains = []
    for n in parts:
        mains.append(refs[at : at + n])
        at += n
    (map_a, map_b, conv_w, conv_b, dt_bias, neg_rate, skip) = refs[at : at + 7]
    (out_ref, wbuf, dt_all, dt_own, xbuf, pbuf, pnext, cbuf, state, wsem, dsem, xsem) = refs[at + 7 :]
    i = pl.program_id(0)
    steps = pl.num_programs(0)
    me_s, me_h = where_ref[0], where_ref[1]
    chans = heads * width
    conv_cols = chans + 2 * state_size
    main_cols = 2 * chans
    map_cols = 2 * state_size
    per = feats // krows
    map_rows = krows + dt_rows * (krows // (2 * state_size))
    me_q = me_s % (shards // 2)

    def move(copy, start):
        if start:
            copy.start()
        else:
            copy.wait()

    def fetch(step, slot, start):
        which = where_ref[2 + step]
        for k in range(shards // 2):
            for inner in (0, 1):
                @pl.when(which == 2 * k + inner)
                def _(k=k, inner=inner):
                    part = pl.ds(inner * rows, rows)
                    for e in range(blocks):
                        beyond, core = divmod(e, 2)
                        array = k + beyond * (shards // 2)
                        if array < many:
                            src, block = gathered[array].at[core, part, :], e
                        else:
                            src, block = last[core].at[part, :], (e & ~1) + ((me_h & 1) ^ core)
                        dst = xbuf.at[slot, :, pl.ds(pl.multiple_of(block * feats, feats), feats)]
                        move(pltpu.make_async_copy(src, dst, xsem.at[slot, e]), start)

    def weights(start):
        for d in range(shards):
            kb = me_s ^ d
            block = kb // per
            place = ((block // 2) ^ (me_h // 2)) * 2 + (block % 2)
            row = pl.multiple_of(place * feats + (kb % per) * krows, krows)
            source, place_row = maps_of[d]
            map_src = (map_a, map_b)[source]
            lo_row = place_row * map_rows
            depth = krows // len(mains[d])
            for n, src in enumerate(mains[d]):
                dst = wbuf.at[pl.ds(row + n * depth, depth), pl.ds(0, main_cols)]
                move(pltpu.make_async_copy(src, dst, wsem.at[n, d]), start)
            dst = wbuf.at[pl.ds(row, krows), pl.ds(main_cols, map_cols)]
            move(pltpu.make_async_copy(map_src.at[pl.ds(lo_row, krows), :], dst, wsem.at[2, d]), start)
            for n in range(krows // map_cols):
                src = map_src.at[pl.ds(lo_row + krows + n * dt_rows, dt_rows), :]
                dst = dt_all.at[:, pl.ds(pl.multiple_of(row + n * map_cols, map_cols), map_cols)]
                move(pltpu.make_async_copy(src, dst, dsem.at[n, d]), start)

    slot = lax.rem(i, 2)
    shard_count = steps - 1

    @pl.when(i == 0)
    def _():
        fetch(0, 0, True)
        weights(True)
        state[...] = jnp.zeros_like(state)
        cbuf[0:8, :] = jnp.zeros((8, conv_cols), jnp.float32)

    @pl.when(i + 1 < shard_count)
    def _():
        fetch(i + 1, 1 - slot, True)

    @pl.when(i == 0)
    def _():
        weights(False)
        own_row = lax.broadcasted_iota(jnp.int32, (LANES, dt_rows), 0)
        group_row = lax.broadcasted_iota(jnp.int32, (LANES, dt_rows), 1)
        mine = (group_row == own_row + me_q * heads) & (own_row < heads)
        pick = jnp.where(mine, 1.0, 0.0).astype(jnp.bfloat16)
        for lo in range(0, dim, feats):
            dt_own[:, lo : lo + feats] = jnp.dot(
                pick, dt_all[:, lo : lo + feats], preferred_element_type=jnp.float32
            ).astype(jnp.bfloat16)

    @pl.when(i < shard_count)
    def _():
        fetch(i, slot, False)

    total = main_cols + map_cols + LANES
    tiles = [(lo, min(256, total - lo)) for lo in range(0, total, 256)]
    length = STRETCH
    stretches = rows // length

    def row_factor():
        squares = jnp.zeros((rows, LANES), jnp.float32)
        for lo in range(0, dim, LANES):
            part = xbuf[slot, :, lo : lo + LANES].astype(jnp.float32)
            squares = squares + part * part
        squares = jnp.sum(squares, axis=1, keepdims=True)
        return lax.rsqrt(squares * (1.0 / dim) + EPS)

    def project(tile, factor):
        lo, cols = tile
        if lo < total - LANES:
            part = jnp.dot(xbuf[slot], wbuf[:, lo : lo + cols], preferred_element_type=jnp.float32)
        else:
            part = lax.dot_general(
                xbuf[slot], dt_own[...], (((1,), (1,)), ((), ())), preferred_element_type=jnp.float32
            )
        pnext[:, lo : lo + cols] = part * factor

    def hand_over():
        pbuf[:, :chans] = pnext[:, :chans]
        pbuf[:, chans:] = pnext[:, total - LANES :]
        cbuf[8 : 8 + rows, :] = pnext[:, chans : chans + conv_cols]

    def constants():
        tri = lax.broadcasted_iota(jnp.int32, (length, length), 0) >= lax.broadcasted_iota(
            jnp.int32, (length, length), 1
        )
        ones = jnp.where(tri, 1.0, 0.0).astype(jnp.bfloat16)
        row = lax.broadcasted_iota(jnp.int32, (2 * LANES, chans), 0) % LANES
        lane = lax.broadcasted_iota(jnp.int32, (2 * LANES, chans), 1) // width
        widen = jnp.where(row == lane, 1.0, 0.0).astype(jnp.bfloat16)
        lane_head = lax.broadcasted_iota(jnp.int32, (1, chans), 1) // width
        masks = [jnp.where(lane_head == j, 1.0, 0.0).astype(jnp.bfloat16) for j in range(heads)]
        return tri, ones, widen, masks

    def scan(st, tri, ones, widen, masks):
        r0 = st * length
        summed = conv_b[...]
        for k in range(taps):
            first = 8 - (taps - 1) + k + r0
            summed = summed + conv_w[k : k + 1, :] * cbuf[first : first + length, :]
        narrow = silu_of(summed).astype(jnp.bfloat16)
        in_map = narrow[:, chans : chans + state_size]
        out_map = narrow[:, chans + state_size :]
        xf = narrow[:, :chans].astype(jnp.float32)
        raw = pbuf[r0 : r0 + length, chans:] + dt_bias[...]
        step = jnp.maximum(raw, 0.0) + jnp.log1p(jnp.exp(-jnp.abs(raw)))
        logd = neg_rate[...] * step
        term0 = logd.astype(jnp.bfloat16)
        rest = logd - term0.astype(jnp.float32)
        term1 = rest.astype(jnp.bfloat16)
        term2 = (rest - term1.astype(jnp.float32)).astype(jnp.bfloat16)
        sums = jnp.dot(ones, jnp.concatenate([term0, term1, term2], axis=1), preferred_element_type=jnp.float32)
        cum = sums[:, :LANES] + (sums[:, LANES : 2 * LANES] + sums[:, 2 * LANES :])
        cum_t = cum.T
        columns = jnp.concatenate([jnp.exp(cum), step, jnp.exp(cum[length - 1 :, :] - cum)], axis=0)
        high = columns.astype(jnp.bfloat16)
        low = (columns - high.astype(jnp.float32)).astype(jnp.bfloat16)
        wide = jnp.dot(jnp.concatenate([high, low], axis=1), widen, preferred_element_type=jnp.float32)
        since, stepped, to_end = wide[:length], wide[length : 2 * length], wide[2 * length :]
        scores = lax.dot_general(
            out_map, in_map, (((1,), (1,)), ((), ())), preferred_element_type=jnp.float32
        )
        scores = jnp.where(tri, scores, 0.0)
        taken = xf * stepped
        taken_low = taken.astype(jnp.bfloat16)
        weighted, spaced = [], []
        for j in range(heads):
            gap = jnp.minimum(cum[:, j : j + 1] - cum_t[j : j + 1, :], 0.0)
            weighted.append((scores * jnp.exp(gap)).astype(jnp.bfloat16))
            spaced.append(taken_low * masks[j])
        within = jnp.dot(
            jnp.concatenate(weighted, axis=1),
            jnp.concatenate(spaced, axis=0),
            preferred_element_type=jnp.float32,
        )
        now = state[...]
        across = jnp.dot(out_map, now.astype(jnp.bfloat16), preferred_element_type=jnp.float32)
        y = within + since * across + skip[...] * xf
        fresh = lax.dot_general(
            in_map, (taken * to_end).astype(jnp.bfloat16), (((0,), (0,)), ((), ())), preferred_element_type=jnp.float32
        )
        state[...] = since[length - 1 :, :] * now + fresh
        gate = pbuf[r0 : r0 + length, :chans]
        out_ref[r0 : r0 + length, :] = (y * silu_of(gate)).astype(jnp.bfloat16)

    def keep_tail():
        cbuf[0:8, :] = cbuf[rows : rows + 8, :]

    @pl.when(i == 0)
    def _():
        factor = row_factor()
        for tile in tiles:
            project(tile, factor)
        hand_over()

    @pl.when((i > 0) & (i < shard_count))
    def _():
        held = constants()
        factor = row_factor()
        for n in range(max(len(tiles), stretches)):
            if n < len(tiles):
                project(tiles[n], factor)
            if n < stretches:
                scan(n, *held)
        keep_tail()
        hand_over()

    @pl.when(i == shard_count)
    def _():
        held = constants()
        for n in range(stretches):
            scan(n, *held)


def mixer(
    where, gathered, last, mains, maps, maps_of, conv_w, conv_b, dt_bias, neg_rate, skip, rows, heads, width, dim
):
    shards = len(mains)
    feats = last[0].shape[1]
    blocks = dim // feats
    krows = mains[0].shape[0]
    chans = heads * width
    state_size = maps[0].shape[1] // 2
    parts = tuple(len(m) if isinstance(m, tuple) else 1 for m in mains)
    dt_rows = heads * shards // 2
    taps = conv_w.shape[0]
    total = 2 * chans + 2 * state_size + LANES
    cfg = (shards, tuple(maps_of), parts, dt_rows, blocks, rows, feats, krows, heads, width, state_size, taps, dim)
    hbm = pl.BlockSpec(memory_space=pl.ANY)

    def whole(a):
        return pl.BlockSpec(a.shape, lambda i, w: (0,) * a.ndim)

    small = (conv_w, conv_b, dt_bias, neg_rate, skip)
    flat_mains = [part for m in mains for part in (m if isinstance(m, tuple) else (m,))]
    large = (*gathered, *last, *flat_mains, *maps)
    return pl.pallas_call(
        partial(mixer_kernel, cfg),
        out_shape=jax.ShapeDtypeStruct((rows * shards, chans), jnp.bfloat16),
        grid_spec=pltpu.PrefetchScalarGridSpec(
            num_scalar_prefetch=1,
            grid=(shards + 1,),
            in_specs=[hbm] * len(large) + [whole(a) for a in small],
            out_specs=pl.BlockSpec((rows, chans), lambda i, w: (jnp.maximum(i - 1, 0), 0)),
            scratch_shapes=[
                pltpu.VMEM((dim, total - LANES), jnp.bfloat16),
                pltpu.VMEM((dt_rows, dim), jnp.bfloat16),
                pltpu.VMEM((LANES, dim), jnp.bfloat16),
                pltpu.VMEM((2, rows, dim), jnp.bfloat16),
                pltpu.VMEM((rows, chans + LANES), jnp.float32),
                pltpu.VMEM((rows, total), jnp.float32),
                pltpu.VMEM((8 + rows, chans + 2 * state_size), jnp.float32),
                pltpu.VMEM((state_size, chans), jnp.float32),
                pltpu.SemaphoreType.DMA((3, shards)),
                pltpu.SemaphoreType.DMA((krows // (2 * state_size), shards)),
                pltpu.SemaphoreType.DMA((2, blocks)),
            ],
        ),
        compiler_params=pltpu.CompilerParams(vmem_limit_bytes=VMEM_LIMIT, dimension_semantics=("arbitrary",)),
        cost_estimate=pl.CostEstimate(
            flops=2 * rows * shards * dim * total, bytes_accessed=2 * rows * shards * dim, transcendentals=0
        ),
    )(where, *large, *small)


def terms_kernel(cfg, where_ref, *refs):
    shards, chans, groups, order, keep = cfg
    count = shards + 1 if keep else 1
    values, w_hbm, outs = refs[:count], refs[count], refs[count + 1 : count + 1 + len(order)]
    w_buf, sem = refs[-2], refs[-1]
    flat = refs[count + 1 + len(order)] if keep else values[0]
    depth, feats = w_buf.shape[1:]
    chunks = sem.shape[1]
    part_rows = depth // chunks
    me_s = where_ref[0]

    def copy(block, n):
        part = pl.ds(n * part_rows, part_rows)
        lane = pl.multiple_of((where_ref[1] ^ order[block]) * feats, feats)
        return pltpu.make_async_copy(
            w_hbm.at[part, pl.ds(lane, feats)], w_buf.at[block, part, :], sem.at[block, n]
        )

    for block in range(len(order)):
        for n in range(chunks):
            copy(block, n).start()
    if keep:
        gated, gain = values[:shards], values[shards]
        per = shards // groups
        for g in range(groups):
            squares = 0.0
            parts = []
            for d in range(g * per, (g + 1) * per):
                part = gated[d][...].astype(jnp.float32)
                parts.append(part)
                squares = squares + jnp.sum(part * part, axis=1, keepdims=True)
            factor = lax.rsqrt(squares * (1.0 / (per * chans)) + EPS)
            for d, part in zip(range(g * per, (g + 1) * per), parts):
                t = me_s ^ d
                value = (part * factor * gain[pl.ds(t, 1), :]).astype(jnp.bfloat16)
                flat[:, pl.ds(pl.multiple_of(t * chans, chans), chans)] = value
    for block, out_ref in enumerate(outs):
        for n in range(chunks):
            copy(block, n).wait()
        for lo in range(0, feats, 256):
            cols = min(256, feats - lo)
            out_ref[:, lo : lo + cols] = jnp.dot(
                flat[...], w_buf[block, :, lo : lo + cols], preferred_element_type=jnp.float32
            ).astype(jnp.bfloat16)


def out_terms(where, values, w_flat, shape, order, keep):
    shards, groups, rows, chans, blocks = shape
    depth, dim = w_flat.shape
    feats = dim // blocks
    vmem = pl.BlockSpec(memory_space=pltpu.VMEM)
    widths = [feats] * len(order) + ([depth] if keep else [])
    out_shape = tuple(jax.ShapeDtypeStruct((rows, n), jnp.bfloat16) for n in widths)
    return pl.pallas_call(
        partial(terms_kernel, (shards, chans, groups, order, keep)),
        out_shape=out_shape,
        in_specs=[pl.BlockSpec(memory_space=pltpu.SMEM)] + [vmem] * len(values) + [pl.BlockSpec(memory_space=pl.ANY)],
        out_specs=(vmem,) * len(widths),
        scratch_shapes=[
            pltpu.VMEM((len(order), depth, feats), jnp.bfloat16),
            pltpu.SemaphoreType.DMA((len(order), 8)),
        ],
        compiler_params=pltpu.CompilerParams(vmem_limit_bytes=VMEM_LIMIT),
        cost_estimate=pl.CostEstimate(
            flops=rows * feats,
            bytes_accessed=rows * feats,
            transcendentals=0,
        ),
    )(where, *values, w_flat)


def line(value, pairs):
    return lax.ppermute(value, "seq", [(2 * a + y, 2 * b + y) for a, b in pairs for y in (0, 1)])


def stack(*parts):
    return jnp.concatenate(parts, axis=0)


def both_cores(value):
    pairs = [[i, i + 1] for i in range(0, lax.axis_size("head"), 2)]
    return lax.all_gather(value, "head", axis=0, axis_index_groups=pairs)


def together(*values):
    return lax.optimization_barrier(values)


def exchange(tokens, w_in, weights_of):
    at = lax.axis_index("seq") // 2
    middle = (at == 1) | (at == 2)
    cross, outward = [(1, 2), (2, 1)], [(1, 0), (2, 3)]

    def x_swap(v):
        return swap(v, "head", 2)

    def s_swap(v, bit):
        return swap(v, "seq", bit)

    xp, y0, z1, c0, (m1, m7, far_map), w_in = together(
        x_swap(tokens),
        s_swap(tokens, 1),
        s_swap(tokens, 2),
        line(tokens, cross),
        weights_of(w_in, (1, 7, "far")),
        w_in,
    )
    xy, yz1, c1, o0, (m2, m6, m5, m4, m3, m0, own_map) = together(
        x_swap(y0),
        s_swap(z1, 1),
        line(z1, cross),
        line(c0, outward),
        weights_of(w_in, (2, 6, 5, 4, 3, 0, "own")),
    )
    q1 = jnp.where(middle, c0, o0)
    q1, z1, yz1, c1, m7, far_map = together(q1, z1, yz1, c1, m7, far_map)
    a1 = stack(z1, yz1)
    xa1, w7, yq1, o1, far_map = together(
        x_swap(a1), s_swap(m7, 7), s_swap(q1, 1), line(c1, outward), s_swap(far_map, 4)
    )
    own = [stack(tokens, y0), a1]
    across = [stack(xp, xy), xa1]
    q2 = jnp.where(middle, c1, o1)
    a2 = stack(q1, yq1)
    maps = stack(own_map, far_map)
    half = m6.shape[0] // 2
    q2, a2, maps, m5, m6a, m6b = together(q2, a2, maps, m5, m6[:half], m6[half:])
    xa2, w5, w6a, yq2, maps_z = together(
        x_swap(a2), s_swap(m5, 5), s_swap(m6a, 6), s_swap(q2, 1), s_swap(maps, 2)
    )
    a3 = stack(q2, yq2)
    maps = stack(maps, maps_z)
    a3, maps, m4, m6b, m3 = together(a3, maps, m4, m6b, m3)
    xa3, w4, w6b, maps_y, w3 = together(
        x_swap(a3), s_swap(m4, 4), s_swap(m6b, 6), s_swap(maps, 1), s_swap(m3, 3)
    )
    own += [a2, a3]
    across += [xa2]
    gathered = [both_cores(v) for v in own + across]
    m1, m2, xa3, w3 = together(m1, m2, xa3, w3)
    w1, w2 = s_swap(m1, 1), s_swap(m2, 2)
    last = (xa3, swap(xa3, "head", 1))
    mains = [m0, w1, w2, w3, w4, w5, (w6a, w6b), w7]
    place = {0: 0, 4: 1, 2: 2, 6: 3}
    maps_of = [(d & 1, place[d & ~1]) for d in range(8)]
    return gathered, last, mains, (maps, maps_y), maps_of


def piece_table(shards):
    me = lax.axis_index("seq")
    shard = jnp.arange(shards)
    outer = (shard // 2) ^ (me // 2)
    middle = (me // 2 == 1) | (me // 2 == 2)
    slot = jnp.where((outer >= 2) & middle, outer ^ 1, outer)
    return slot * 2 + ((shard ^ me) & 1)


def head_split_body(
    tokens, norm_gain, w_in, w_dt, dt_bias, a_log, d_skip, conv_w, conv_b, gate_gain, w_out
):
    shards, blocks = lax.axis_size("seq"), lax.axis_size("head")
    s, h = lax.axis_index("seq"), lax.axis_index("head")
    rows = tokens.shape[0]
    krows, groups, wide = w_in.shape
    group_width = gate_gain.shape[1]
    state_size = (conv_b.shape[1] - group_width) // 2
    local_heads = dt_bias.shape[0]
    heads = local_heads // shards
    width = groups * group_width // local_heads
    chans = heads * width
    per = shards // groups
    dim = krows * shards

    gain = lax.dynamic_slice_in_dim(norm_gain, s * krows, krows, 0)

    dt_cols = local_heads // groups

    def weights_of(w_in, names):
        def columns(t, first, count):
            part = lax.dynamic_slice(w_in, (0, t // per, first), (krows, 1, count))[:, 0]
            return (part.astype(jnp.float32) * gain[:, None]).astype(jnp.bfloat16)

        def one(name):
            if name in ("far", "own"):
                t = s ^ per if name == "far" else s
                dt = lax.dynamic_slice_in_dim(w_dt, (t // per) * dt_cols, dt_cols, 1).T
                dt = (dt.astype(jnp.float32) * gain[None, :]).astype(jnp.bfloat16)
                cols = 2 * state_size
                rows_of_dt = [dt[:, lo : lo + cols] for lo in range(0, krows, cols)]
                return jnp.concatenate([columns(t, 2 * group_width, cols), *rows_of_dt], axis=0)
            t = s ^ name
            first = (t % per) * chans
            return jnp.concatenate(
                [columns(t, first, chans), columns(t, group_width + first, chans)], axis=1
            )

        return tuple(one(name) for name in names)

    gathered, last, mains, maps, maps_of = exchange(tokens, w_in, weights_of)

    group = s // per
    quarter = (s % per) * chans

    def own_channels(a):
        a = lax.dynamic_index_in_dim(a, group, a.ndim - 2, keepdims=False)
        inputs = lax.dynamic_slice_in_dim(a, quarter, chans, a.ndim - 1)
        return jnp.concatenate([inputs, a[..., group_width:]], axis=-1)

    def own_heads(a):
        return lax.dynamic_slice_in_dim(a, s * heads, heads, 0)

    def lanes(a):
        return jnp.pad(a, (0, LANES - heads))[None, :]

    where = jnp.concatenate([jnp.stack([s, h]), piece_table(shards)]).astype(jnp.int32)
    gated = mixer(
        where,
        gathered,
        last,
        mains,
        maps,
        maps_of,
        own_channels(conv_w),
        own_channels(conv_b)[None, :],
        lanes(own_heads(dt_bias)),
        lanes(-jnp.exp(own_heads(a_log))),
        jnp.repeat(own_heads(d_skip), width)[None, :],
        rows,
        heads,
        width,
        dim,
    )
    blocks_out = [
        lax.dynamic_slice_in_dim(gated, (s ^ d) * rows, rows, 0) for d in range(shards)
    ]
    arrived = [blocks_out[0]] + [None] * (shards - 1)
    for d in range(shards - 1, 0, -1):
        arrived[d] = swap(blocks_out[d], "seq", d)

    gains = gate_gain.reshape(shards, chans)
    w_flat = w_out.reshape(groups * group_width, w_out.shape[2])
    wide = jnp.float32
    shape = (shards, groups, rows, chans, blocks)
    shape = (shards, groups, rows, chans, blocks)
    first, third, flat = out_terms(where, [*arrived, gains], w_flat, shape, (3, 1), True)
    via_core, from_core = swap(first, "head", 1), swap(third, "head", 1)
    (second,) = out_terms(where, [flat], w_flat, shape, (2,), False)
    to_pair, flat = together((second.astype(wide) + via_core.astype(wide)).astype(jnp.bfloat16), flat)
    beyond = swap(to_pair, "head", 2)
    (own,) = out_terms(where, [flat], w_flat, shape, (0,), False)
    return (own.astype(wide) + from_core.astype(wide) + beyond.astype(wide)).astype(jnp.bfloat16)


def fits_head_split(mesh, w_in, gate_gain, dt_bias):
    shards, blocks = mesh.shape["seq"], mesh.shape["head"]
    groups = gate_gain.shape[0] // blocks
    local_heads = dt_bias.shape[0] // blocks
    chans = groups * gate_gain.shape[1] // shards
    return shards == 8 and blocks == 4 and groups == 2 and local_heads % shards == 0 and chans % LANES == 0


def from_behind(shard, axis, by):
    count = lax.axis_size(axis)
    pairs = [(i, i + by) for i in range(count) if 0 <= i + by < count]
    return lax.ppermute(shard, axis, pairs)


def carried_in(shard, axis, combine, identity):
    count, index = (lax.axis_size(axis), lax.axis_index(axis))
    everything = jax.tree.map(
        lambda part, kind: lax.all_gather(part.astype(kind), axis),
        shard,
        (jnp.bfloat16, jnp.bfloat16),
    )
    start = jax.tree.map(
        lambda part, zero: jnp.broadcast_to(jnp.asarray(zero, part.dtype), part.shape),
        shard,
        identity,
    )

    def lap(k, before):
        reached = k < index
        new = combine(
            before, jax.tree.map(lambda part, own: part[k].astype(own.dtype), everything, shard)
        )
        return jax.tree.map(lambda a, b: jnp.where(reached, a, b), new, before)

    return lax.fori_loop(0, count, lap, start)


def normalize(values, gain):
    squares = jnp.mean(values * values, axis=-1, keepdims=True)
    return values * lax.rsqrt(squares + EPS) * gain


def state_block(inputs, step_size, log_decay, in_map, out_map, block_len):
    length = inputs.shape[0]
    stretch_count = length // block_len
    head_count = inputs.shape[1]
    head_size = inputs.shape[2]
    state_size = in_map.shape[1]
    shaped = (
        inputs.reshape(stretch_count, block_len, head_count, head_size),
        step_size.reshape(stretch_count, block_len, head_count),
        log_decay.reshape(stretch_count, block_len, head_count),
        in_map.reshape(stretch_count, block_len, state_size),
        out_map.reshape(stretch_count, block_len, state_size),
    )
    causal = jnp.arange(block_len)[:, None] >= jnp.arange(block_len)[None, :]

    def advance(state_now, pieces):
        stretch_in, stretch_step, stretch_log, stretch_b, stretch_c = pieces
        cumulative = jnp.cumsum(stretch_log, axis=0)
        gap_log = cumulative[:, None, :] - cumulative[None, :, :]
        decays = jnp.where(
            causal[:, :, None], jnp.exp(jnp.where(causal[:, :, None], gap_log, 0.0)), 0.0
        )
        scores = jnp.dot(stretch_c, stretch_b.T, preferred_element_type=jnp.float32)
        wide_c = stretch_c.astype(jnp.float32)
        wide_b = stretch_b.astype(jnp.float32)
        weights = scores[:, :, None] * decays * stretch_step[None, :, :]
        within = jnp.einsum("ijh,jhp->ihp", weights, stretch_in, precision=HIGHEST)
        across = jnp.exp(cumulative)[:, :, None] * jnp.einsum(
            "in,hpn->ihp", wide_c, state_now, precision=HIGHEST
        )
        to_end = jnp.exp(cumulative[-1][None, :] - cumulative) * stretch_step
        fresh_state = jnp.einsum("jh,jhp,jn->hpn", to_end, stretch_in, wide_b, precision=HIGHEST)
        state_next = jnp.exp(cumulative[-1])[:, None, None] * state_now + fresh_state
        return (state_next, within + across)

    start_state = jnp.zeros((head_count, head_size, state_size), jnp.float32)
    final, outputs = lax.scan(advance, start_state, shaped)
    return (outputs.reshape(length, head_count, head_size), final)


def link_states(earlier, later):
    return (earlier[0] + later[0], jnp.exp(later[0])[:, :, None, None] * earlier[1] + later[1])


def sequence_split_body(tokens, norm_gain, w_in, w_dt, dt_bias, a_log, d_skip, conv_w, conv_b, gate_gain, w_out):
    local_rows = tokens.shape[0]
    kernel_len = conv_w.shape[0]
    groups, group_width = gate_gain.shape
    head_count = dt_bias.shape[0]
    per_group = head_count // groups
    head_size = group_width // per_group
    state_size = (conv_b.shape[1] - group_width) // 2
    gathered = lax.all_gather(tokens, "head", axis=1, tiled=True)
    normed = normalize(gathered.astype(jnp.float32), norm_gain).astype(jnp.bfloat16)
    span_rows = normed.shape[0]
    flat_in = w_in.reshape(w_in.shape[0], groups * w_in.shape[2])
    proj_sum = jnp.dot(
        normed,
        lax.all_gather(flat_in, "seq", axis=0, tiled=True),
        preferred_element_type=jnp.float32,
    )
    step_sum = jnp.dot(
        normed, lax.all_gather(w_dt, "seq", axis=0, tiled=True), preferred_element_type=jnp.float32
    )
    projected = proj_sum.astype(jnp.bfloat16).reshape(span_rows, groups, w_in.shape[2])
    step_size = jax.nn.softplus(step_sum + dt_bias[None, :])
    gate_raw = projected[span_rows - local_rows :, :, :group_width]
    own_channels = projected[:, :, group_width:]
    rim_rows = from_behind(own_channels[local_rows - kernel_len + 1 :], "seq", 1)
    extended = jnp.concatenate([rim_rows, own_channels], axis=0)
    summed = conv_b[None, :, :]
    for offset in range(kernel_len):
        summed = summed + conv_w[offset][None, :, :] * extended[
            offset : offset + local_rows
        ].astype(jnp.float32)
    narrow = lax.optimization_barrier(jax.nn.silu(summed).astype(jnp.bfloat16))
    convolved = narrow.astype(jnp.float32)
    inputs = convolved[:, :, :group_width].reshape(local_rows, groups, per_group, head_size)
    in_map = narrow[:, :, group_width : group_width + state_size]
    out_map = narrow[:, :, group_width + state_size :]
    step_grouped = step_size.reshape(local_rows, groups, per_group)
    log_decay = -jnp.exp(a_log).reshape(groups, per_group)[None, :, :] * step_grouped
    run_block = jax.vmap(
        partial(state_block, block_len=STRETCH), in_axes=(1, 1, 1, 1, 1), out_axes=(1, 0)
    )
    local_out, ending = run_block(inputs, step_grouped, log_decay, in_map, out_map)
    totals = jnp.sum(log_decay, axis=0)
    identity = (jnp.zeros_like(totals), jnp.zeros_like(ending))
    prior_decay, incoming = carried_in((totals, ending), "seq", link_states, identity)
    cumulative = jnp.exp(jnp.cumsum(log_decay, axis=0))
    carried = (
        jnp.einsum("tgn,ghpn->tghp", out_map.astype(jnp.float32), incoming, precision=HIGHEST)
        * cumulative[:, :, :, None]
    )
    outputs = local_out + carried + d_skip.reshape(groups, per_group)[None, :, :, None] * inputs
    gated = outputs.reshape(local_rows, groups, group_width) * jax.nn.silu(
        gate_raw.astype(jnp.float32)
    )
    normed_out = normalize(gated, gate_gain[None, :, :]).astype(jnp.bfloat16)
    flat_out = normed_out.reshape(local_rows, groups * group_width)
    terms = jnp.dot(
        flat_out,
        w_out.reshape(groups * group_width, w_out.shape[2]),
        preferred_element_type=jnp.float32,
    )
    return lax.psum_scatter(terms.astype(jnp.bfloat16), "head", scatter_dimension=1, tiled=True)


def solution(mesh):
    in_specs = (
        P("seq", "head"),
        P(),
        P("seq", "head", None),
        P("seq", "head"),
        P("head"),
        P("head"),
        P("head"),
        P(None, "head", None),
        P("head", None),
        P("head", None),
        P("head", None, None),
    )
    out_specs = P("seq", "head")

    def mixer_prefill(*args):
        by_heads = fits_head_split(mesh, args[2], args[9], args[4])
        body = head_split_body if by_heads else sequence_split_body
        mapped = jax.shard_map(
            body, mesh=mesh, in_specs=in_specs, out_specs=out_specs, check_vma=False
        )
        return mapped(*args)

    return mixer_prefill
```

```python
from functools import partial

import jax
import jax.numpy as jnp
from jax import lax
from jax.experimental import pallas as pl
from jax.experimental.pallas import tpu as pltpu
from jax.sharding import PartitionSpec as P

STRETCH = 128


EPS = 1e-05
HIGHEST = lax.Precision.HIGHEST
VMEM_LIMIT = 58 * 1024 * 1024
LANES = 128


def swap(value, axis, bit):
    count = lax.axis_size(axis)
    return lax.ppermute(value, axis, [(i, i ^ bit) for i in range(count)])


def silu_of(v):
    half = 0.5 * v
    return half + half * jnp.tanh(half)


def mixer_kernel(
    cfg,
    where_ref,
    *refs,
):
    (shards, maps_of, parts, dt_rows, blocks, rows, feats, krows, heads, width, state_size, taps, dim) = cfg
    many = shards - 1
    gathered, last = refs[:many], refs[many : many + 2]
    at = many + 2
    mains = []
    for n in parts:
        mains.append(refs[at : at + n])
        at += n
    (map_a, map_b, conv_w, conv_b, dt_bias, neg_rate, skip) = refs[at : at + 7]
    (out_ref, wbuf, dt_all, dt_own, xbuf, pbuf, pnext, cbuf, state, wsem, dsem, xsem) = refs[at + 7 :]
    i = pl.program_id(0)
    steps = pl.num_programs(0)
    me_s, me_h = where_ref[0], where_ref[1]
    chans = heads * width
    conv_cols = chans + 2 * state_size
    main_cols = 2 * chans
    map_cols = 2 * state_size
    per = feats // krows
    map_rows = krows + dt_rows * (krows // (2 * state_size))
    me_q = me_s % (shards // 2)

    def move(copy, start):
        if start:
            copy.start()
        else:
            copy.wait()

    def fetch(step, slot, start):
        which = where_ref[2 + step]
        for k in range(shards // 2):
            for inner in (0, 1):
                @pl.when(which == 2 * k + inner)
                def _(k=k, inner=inner):
                    part = pl.ds(inner * rows, rows)
                    for e in range(blocks):
                        beyond, core = divmod(e, 2)
                        array = k + beyond * (shards // 2)
                        if array < many:
                            src, block = gathered[array].at[core, part, :], e
                        else:
                            src, block = last[core].at[part, :], (e & ~1) + ((me_h & 1) ^ core)
                        dst = xbuf.at[slot, :, pl.ds(pl.multiple_of(block * feats, feats), feats)]
                        move(pltpu.make_async_copy(src, dst, xsem.at[slot, e]), start)

    def weights(start):
        for d in range(shards):
            kb = me_s ^ d
            block = kb // per
            place = ((block // 2) ^ (me_h // 2)) * 2 + (block % 2)
            row = pl.multiple_of(place * feats + (kb % per) * krows, krows)
            source, place_row = maps_of[d]
            map_src = (map_a, map_b)[source]
            lo_row = place_row * map_rows
            depth = krows // len(mains[d])
            for n, src in enumerate(mains[d]):
                dst = wbuf.at[pl.ds(row + n * depth, depth), pl.ds(0, main_cols)]
                move(pltpu.make_async_copy(src, dst, wsem.at[n, d]), start)
            dst = wbuf.at[pl.ds(row, krows), pl.ds(main_cols, map_cols)]
            move(pltpu.make_async_copy(map_src.at[pl.ds(lo_row, krows), :], dst, wsem.at[2, d]), start)
            for n in range(krows // map_cols):
                src = map_src.at[pl.ds(lo_row + krows + n * dt_rows, dt_rows), :]
                dst = dt_all.at[:, pl.ds(pl.multiple_of(row + n * map_cols, map_cols), map_cols)]
                move(pltpu.make_async_copy(src, dst, dsem.at[n, d]), start)

    slot = lax.rem(i, 2)
    shard_count = steps - 1

    @pl.when(i == 0)
    def _():
        fetch(0, 0, True)
        weights(True)
        state[...] = jnp.zeros_like(state)
        cbuf[0:8, :] = jnp.zeros((8, conv_cols), jnp.float32)

    @pl.when(i + 1 < shard_count)
    def _():
        fetch(i + 1, 1 - slot, True)

    @pl.when(i == 0)
    def _():
        weights(False)
        own_row = lax.broadcasted_iota(jnp.int32, (LANES, dt_rows), 0)
        group_row = lax.broadcasted_iota(jnp.int32, (LANES, dt_rows), 1)
        mine = (group_row == own_row + me_q * heads) & (own_row < heads)
        pick = jnp.where(mine, 1.0, 0.0).astype(jnp.bfloat16)
        for lo in range(0, dim, feats):
            dt_own[:, lo : lo + feats] = jnp.dot(
                pick, dt_all[:, lo : lo + feats], preferred_element_type=jnp.float32
            ).astype(jnp.bfloat16)

    @pl.when(i < shard_count)
    def _():
        fetch(i, slot, False)

    total = main_cols + map_cols + LANES
    tiles = [(lo, min(256, total - lo)) for lo in range(0, total, 256)]
    length = STRETCH
    stretches = rows // length

    def row_factor():
        squares = jnp.zeros((rows, LANES), jnp.float32)
        for lo in range(0, dim, LANES):
            part = xbuf[slot, :, lo : lo + LANES].astype(jnp.float32)
            squares = squares + part * part
        squares = jnp.sum(squares, axis=1, keepdims=True)
        return lax.rsqrt(squares * (1.0 / dim) + EPS)

    def project(tile, factor):
        lo, cols = tile
        if lo < total - LANES:
            part = jnp.dot(xbuf[slot], wbuf[:, lo : lo + cols], preferred_element_type=jnp.float32)
        else:
            part = lax.dot_general(
                xbuf[slot], dt_own[...], (((1,), (1,)), ((), ())), preferred_element_type=jnp.float32
            )
        pnext[:, lo : lo + cols] = part * factor

    def hand_over():
        pbuf[:, :chans] = pnext[:, :chans]
        pbuf[:, chans:] = pnext[:, total - LANES :]
        cbuf[8 : 8 + rows, :] = pnext[:, chans : chans + conv_cols]

    def constants():
        tri = lax.broadcasted_iota(jnp.int32, (length, length), 0) >= lax.broadcasted_iota(
            jnp.int32, (length, length), 1
        )
        ones = jnp.where(tri, 1.0, 0.0).astype(jnp.bfloat16)
        row = lax.broadcasted_iota(jnp.int32, (2 * LANES, chans), 0) % LANES
        lane = lax.broadcasted_iota(jnp.int32, (2 * LANES, chans), 1) // width
        widen = jnp.where(row == lane, 1.0, 0.0).astype(jnp.bfloat16)
        lane_head = lax.broadcasted_iota(jnp.int32, (1, chans), 1) // width
        masks = [jnp.where(lane_head == j, 1.0, 0.0).astype(jnp.bfloat16) for j in range(heads)]
        return tri, ones, widen, masks

    def scan(st, tri, ones, widen, masks):
        r0 = st * length
        summed = conv_b[...]
        for k in range(taps):
            first = 8 - (taps - 1) + k + r0
            summed = summed + conv_w[k : k + 1, :] * cbuf[first : first + length, :]
        narrow = silu_of(summed).astype(jnp.bfloat16)
        in_map = narrow[:, chans : chans + state_size]
        out_map = narrow[:, chans + state_size :]
        xf = narrow[:, :chans].astype(jnp.float32)
        raw = pbuf[r0 : r0 + length, chans:] + dt_bias[...]
        step = jnp.maximum(raw, 0.0) + jnp.log1p(jnp.exp(-jnp.abs(raw)))
        logd = neg_rate[...] * step
        term0 = logd.astype(jnp.bfloat16)
        rest = logd - term0.astype(jnp.float32)
        term1 = rest.astype(jnp.bfloat16)
        term2 = (rest - term1.astype(jnp.float32)).astype(jnp.bfloat16)
        sums = jnp.dot(ones, jnp.concatenate([term0, term1, term2], axis=1), preferred_element_type=jnp.float32)
        cum = sums[:, :LANES] + (sums[:, LANES : 2 * LANES] + sums[:, 2 * LANES :])
        cum_t = cum.T
        columns = jnp.concatenate([jnp.exp(cum), step, jnp.exp(cum[length - 1 :, :] - cum)], axis=0)
        high = columns.astype(jnp.bfloat16)
        low = (columns - high.astype(jnp.float32)).astype(jnp.bfloat16)
        wide = jnp.dot(jnp.concatenate([high, low], axis=1), widen, preferred_element_type=jnp.float32)
        since, stepped, to_end = wide[:length], wide[length : 2 * length], wide[2 * length :]
        scores = lax.dot_general(
            out_map, in_map, (((1,), (1,)), ((), ())), preferred_element_type=jnp.float32
        )
        scores = jnp.where(tri, scores, 0.0)
        taken = xf * stepped
        taken_low = taken.astype(jnp.bfloat16)
        weighted, spaced = [], []
        for j in range(heads):
            gap = jnp.minimum(cum[:, j : j + 1] - cum_t[j : j + 1, :], 0.0)
            weighted.append((scores * jnp.exp(gap)).astype(jnp.bfloat16))
            spaced.append(taken_low * masks[j])
        within = jnp.dot(
            jnp.concatenate(weighted, axis=1),
            jnp.concatenate(spaced, axis=0),
            preferred_element_type=jnp.float32,
        )
        now = state[...]
        across = jnp.dot(out_map, now.astype(jnp.bfloat16), preferred_element_type=jnp.float32)
        y = within + since * across + skip[...] * xf
        fresh = lax.dot_general(
            in_map, (taken * to_end).astype(jnp.bfloat16), (((0,), (0,)), ((), ())), preferred_element_type=jnp.float32
        )
        state[...] = since[length - 1 :, :] * now + fresh
        gate = pbuf[r0 : r0 + length, :chans]
        out_ref[r0 : r0 + length, :] = (y * silu_of(gate)).astype(jnp.bfloat16)

    def keep_tail():
        cbuf[0:8, :] = cbuf[rows : rows + 8, :]

    @pl.when(i == 0)
    def _():
        factor = row_factor()
        for tile in tiles:
            project(tile, factor)
        hand_over()

    @pl.when((i > 0) & (i < shard_count))
    def _():
        held = constants()
        factor = row_factor()
        for n in range(max(len(tiles), stretches)):
            if n < len(tiles):
                project(tiles[n], factor)
            if n < stretches:
                scan(n, *held)
        keep_tail()
        hand_over()

    @pl.when(i == shard_count)
    def _():
        held = constants()
        for n in range(stretches):
            scan(n, *held)


def mixer(
    where, gathered, last, mains, maps, maps_of, conv_w, conv_b, dt_bias, neg_rate, skip, rows, heads, width, dim
):
    shards = len(mains)
    feats = last[0].shape[1]
    blocks = dim // feats
    krows = mains[0].shape[0]
    chans = heads * width
    state_size = maps[0].shape[1] // 2
    parts = tuple(len(m) if isinstance(m, tuple) else 1 for m in mains)
    dt_rows = heads * shards // 2
    taps = conv_w.shape[0]
    total = 2 * chans + 2 * state_size + LANES
    cfg = (shards, tuple(maps_of), parts, dt_rows, blocks, rows, feats, krows, heads, width, state_size, taps, dim)
    hbm = pl.BlockSpec(memory_space=pl.ANY)

    def whole(a):
        return pl.BlockSpec(a.shape, lambda i, w: (0,) * a.ndim)

    small = (conv_w, conv_b, dt_bias, neg_rate, skip)
    flat_mains = [part for m in mains for part in (m if isinstance(m, tuple) else (m,))]
    large = (*gathered, *last, *flat_mains, *maps)
    return pl.pallas_call(
        partial(mixer_kernel, cfg),
        out_shape=jax.ShapeDtypeStruct((rows * shards, chans), jnp.bfloat16),
        grid_spec=pltpu.PrefetchScalarGridSpec(
            num_scalar_prefetch=1,
            grid=(shards + 1,),
            in_specs=[hbm] * len(large) + [whole(a) for a in small],
            out_specs=pl.BlockSpec((rows, chans), lambda i, w: (jnp.maximum(i - 1, 0), 0)),
            scratch_shapes=[
                pltpu.VMEM((dim, total - LANES), jnp.bfloat16),
                pltpu.VMEM((dt_rows, dim), jnp.bfloat16),
                pltpu.VMEM((LANES, dim), jnp.bfloat16),
                pltpu.VMEM((2, rows, dim), jnp.bfloat16),
                pltpu.VMEM((rows, chans + LANES), jnp.float32),
                pltpu.VMEM((rows, total), jnp.float32),
                pltpu.VMEM((8 + rows, chans + 2 * state_size), jnp.float32),
                pltpu.VMEM((state_size, chans), jnp.float32),
                pltpu.SemaphoreType.DMA((3, shards)),
                pltpu.SemaphoreType.DMA((krows // (2 * state_size), shards)),
                pltpu.SemaphoreType.DMA((2, blocks)),
            ],
        ),
        compiler_params=pltpu.CompilerParams(vmem_limit_bytes=VMEM_LIMIT, dimension_semantics=("arbitrary",)),
        cost_estimate=pl.CostEstimate(
            flops=2 * rows * shards * dim * total, bytes_accessed=2 * rows * shards * dim, transcendentals=0
        ),
    )(where, *large, *small)


def terms_kernel(cfg, where_ref, *refs):
    shards, chans, groups, order, keep, added = cfg
    count = shards + 1 if keep else 1 + added
    values, w_hbm, outs = refs[:count], refs[count], refs[count + 1 : count + 1 + len(order)]
    w_buf, sem = refs[-2], refs[-1]
    flat = refs[count + 1 + len(order)] if keep else values[0]
    depth, feats = w_buf.shape[1:]
    chunks = sem.shape[1]
    part_rows = depth // chunks
    me_s = where_ref[0]

    def copy(block, n):
        part = pl.ds(n * part_rows, part_rows)
        lane = pl.multiple_of((where_ref[1] ^ order[block]) * feats, feats)
        return pltpu.make_async_copy(
            w_hbm.at[part, pl.ds(lane, feats)], w_buf.at[block, part, :], sem.at[block, n]
        )

    for block in range(len(order)):
        for n in range(chunks):
            copy(block, n).start()
    if keep:
        gated, gain = values[:shards], values[shards]
        per = shards // groups
        for g in range(groups):
            squares = 0.0
            parts = []
            for d in range(g * per, (g + 1) * per):
                part = gated[d][...].astype(jnp.float32)
                parts.append(part)
                squares = squares + jnp.sum(part * part, axis=1, keepdims=True)
            factor = lax.rsqrt(squares * (1.0 / (per * chans)) + EPS)
            for d, part in zip(range(g * per, (g + 1) * per), parts):
                t = me_s ^ d
                value = (part * factor * gain[pl.ds(t, 1), :]).astype(jnp.bfloat16)
                flat[:, pl.ds(pl.multiple_of(t * chans, chans), chans)] = value
    for block, out_ref in enumerate(outs):
        for n in range(chunks):
            copy(block, n).wait()
        for lo in range(0, feats, 256):
            cols = min(256, feats - lo)
            part = jnp.dot(flat[...], w_buf[block, :, lo : lo + cols], preferred_element_type=jnp.float32)
            if added:
                part = part + values[1][:, lo : lo + cols].astype(jnp.float32)
            out_ref[:, lo : lo + cols] = part.astype(out_ref.dtype)


def out_terms(where, values, w_flat, shape, order, keep=False, kind=jnp.bfloat16):
    shards, groups, rows, chans, blocks = shape
    depth, dim = w_flat.shape
    feats = dim // blocks
    vmem = pl.BlockSpec(memory_space=pltpu.VMEM)
    widths = [feats] * len(order) + ([depth] if keep else [])
    added = 0 if keep else len(values) - 1
    out_shape = tuple(jax.ShapeDtypeStruct((rows, n), kind) for n in widths)
    return pl.pallas_call(
        partial(terms_kernel, (shards, chans, groups, order, keep, added)),
        out_shape=out_shape,
        in_specs=[pl.BlockSpec(memory_space=pltpu.SMEM)] + [vmem] * len(values) + [pl.BlockSpec(memory_space=pl.ANY)],
        out_specs=(vmem,) * len(widths),
        scratch_shapes=[
            pltpu.VMEM((len(order), depth, feats), jnp.bfloat16),
            pltpu.SemaphoreType.DMA((len(order), 8)),
        ],
        compiler_params=pltpu.CompilerParams(vmem_limit_bytes=VMEM_LIMIT),
        cost_estimate=pl.CostEstimate(
            flops=rows * feats,
            bytes_accessed=rows * feats,
            transcendentals=0,
        ),
    )(where, *values, w_flat)


def line(value, pairs):
    return lax.ppermute(value, "seq", [(2 * a + y, 2 * b + y) for a, b in pairs for y in (0, 1)])


def stack(*parts):
    return jnp.concatenate(parts, axis=0)


def both_cores(value):
    pairs = [[i, i + 1] for i in range(0, lax.axis_size("head"), 2)]
    return lax.all_gather(value, "head", axis=0, axis_index_groups=pairs)


def together(*values):
    return lax.optimization_barrier(values)


def exchange(tokens, w_in, weights_of):
    at = lax.axis_index("seq") // 2
    middle = (at == 1) | (at == 2)
    cross, outward = [(1, 2), (2, 1)], [(1, 0), (2, 3)]

    def x_swap(v):
        return swap(v, "head", 2)

    def s_swap(v, bit):
        return swap(v, "seq", bit)

    xp, y0, z1, c0, (m1, m7, far_map), w_in = together(
        x_swap(tokens),
        s_swap(tokens, 1),
        s_swap(tokens, 2),
        line(tokens, cross),
        weights_of(w_in, (1, 7, "far")),
        w_in,
    )
    xy, yz1, c1, o0, (m2, m6, m5, m4, m3, m0, own_map) = together(
        x_swap(y0),
        s_swap(z1, 1),
        line(z1, cross),
        line(c0, outward),
        weights_of(w_in, (2, 6, 5, 4, 3, 0, "own")),
    )
    q1 = jnp.where(middle, c0, o0)
    q1, z1, yz1, c1, m7, far_map = together(q1, z1, yz1, c1, m7, far_map)
    xz1, xyz1, w7, yq1, o1, far_map = together(
        x_swap(z1), x_swap(yz1), s_swap(m7, 7), s_swap(q1, 1), line(c1, outward), s_swap(far_map, 4)
    )
    own = [stack(tokens, y0), stack(z1, yz1)]
    across = [stack(xp, xy), stack(xz1, xyz1)]
    q2 = jnp.where(middle, c1, o1)
    maps = stack(own_map, far_map)
    half = m6.shape[0] // 2
    q2, q1, yq1, maps, m5, m6a, m6b = together(q2, q1, yq1, maps, m5, m6[:half], m6[half:])
    xq1, xyq1, w5, w6a, yq2, maps_z = together(
        x_swap(q1), x_swap(yq1), s_swap(m5, 5), s_swap(m6a, 6), s_swap(q2, 1), s_swap(maps, 2)
    )
    maps = stack(maps, maps_z)
    q2, yq2, maps, m4, m6b, m3 = together(q2, yq2, maps, m4, m6b, m3)
    xq2, xyq2, w4, w6b, maps_y, w3 = together(
        x_swap(q2), x_swap(yq2), s_swap(m4, 4), s_swap(m6b, 6), s_swap(maps, 1), s_swap(m3, 3)
    )
    own += [stack(q1, yq1), stack(q2, yq2)]
    across += [stack(xq1, xyq1)]
    xa3 = stack(xq2, xyq2)
    gathered = [both_cores(v) for v in own + across]
    m1, m2, xa3, w3 = together(m1, m2, xa3, w3)
    w1, w2 = s_swap(m1, 1), s_swap(m2, 2)
    last = (xa3, swap(xa3, "head", 1))
    mains = [m0, w1, w2, w3, w4, w5, (w6a, w6b), w7]
    place = {0: 0, 4: 1, 2: 2, 6: 3}
    maps_of = [(d & 1, place[d & ~1]) for d in range(8)]
    return gathered, last, mains, (maps, maps_y), maps_of


def piece_table(shards):
    me = lax.axis_index("seq")
    shard = jnp.arange(shards)
    outer = (shard // 2) ^ (me // 2)
    middle = (me // 2 == 1) | (me // 2 == 2)
    slot = jnp.where((outer >= 2) & middle, outer ^ 1, outer)
    return slot * 2 + ((shard ^ me) & 1)


def head_split_body(
    tokens, norm_gain, w_in, w_dt, dt_bias, a_log, d_skip, conv_w, conv_b, gate_gain, w_out
):
    shards, blocks = lax.axis_size("seq"), lax.axis_size("head")
    s, h = lax.axis_index("seq"), lax.axis_index("head")
    rows = tokens.shape[0]
    krows, groups, wide = w_in.shape
    group_width = gate_gain.shape[1]
    state_size = (conv_b.shape[1] - group_width) // 2
    local_heads = dt_bias.shape[0]
    heads = local_heads // shards
    width = groups * group_width // local_heads
    chans = heads * width
    per = shards // groups
    dim = krows * shards

    gain = lax.dynamic_slice_in_dim(norm_gain, s * krows, krows, 0)

    dt_cols = local_heads // groups

    def weights_of(w_in, names):
        def columns(t, first, count):
            part = lax.dynamic_slice(w_in, (0, t // per, first), (krows, 1, count))[:, 0]
            return (part.astype(jnp.float32) * gain[:, None]).astype(jnp.bfloat16)

        def one(name):
            if name in ("far", "own"):
                t = s ^ per if name == "far" else s
                dt = lax.dynamic_slice_in_dim(w_dt, (t // per) * dt_cols, dt_cols, 1).T
                dt = (dt.astype(jnp.float32) * gain[None, :]).astype(jnp.bfloat16)
                cols = 2 * state_size
                rows_of_dt = [dt[:, lo : lo + cols] for lo in range(0, krows, cols)]
                return jnp.concatenate([columns(t, 2 * group_width, cols), *rows_of_dt], axis=0)
            t = s ^ name
            first = (t % per) * chans
            return jnp.concatenate(
                [columns(t, first, chans), columns(t, group_width + first, chans)], axis=1
            )

        return tuple(one(name) for name in names)

    gathered, last, mains, maps, maps_of = exchange(tokens, w_in, weights_of)

    group = s // per
    quarter = (s % per) * chans

    def own_channels(a):
        a = lax.dynamic_index_in_dim(a, group, a.ndim - 2, keepdims=False)
        inputs = lax.dynamic_slice_in_dim(a, quarter, chans, a.ndim - 1)
        return jnp.concatenate([inputs, a[..., group_width:]], axis=-1)

    def own_heads(a):
        return lax.dynamic_slice_in_dim(a, s * heads, heads, 0)

    def lanes(a):
        return jnp.pad(a, (0, LANES - heads))[None, :]

    where = jnp.concatenate([jnp.stack([s, h]), piece_table(shards)]).astype(jnp.int32)
    gated = mixer(
        where,
        gathered,
        last,
        mains,
        maps,
        maps_of,
        own_channels(conv_w),
        own_channels(conv_b)[None, :],
        lanes(own_heads(dt_bias)),
        lanes(-jnp.exp(own_heads(a_log))),
        jnp.repeat(own_heads(d_skip), width)[None, :],
        rows,
        heads,
        width,
        dim,
    )
    blocks_out = [
        lax.dynamic_slice_in_dim(gated, (s ^ d) * rows, rows, 0) for d in range(shards)
    ]
    arrived = [blocks_out[0]] + [None] * (shards - 1)
    for d in range(shards - 1, 0, -1):
        arrived[d] = swap(blocks_out[d], "seq", d)

    gains = gate_gain.reshape(shards, chans)
    w_flat = w_out.reshape(groups * group_width, w_out.shape[2])
    shape = (shards, groups, rows, chans, blocks)
    shape = (shards, groups, rows, chans, blocks)
    first, third, flat = out_terms(where, [*arrived, gains], w_flat, shape, (3, 1), True)
    via_core, from_core = swap(first, "head", 1), swap(third, "head", 1)
    (to_pair,) = out_terms(where, [flat, via_core], w_flat, shape, (2,))
    to_pair, flat = together(to_pair, flat)
    beyond = swap(to_pair, "head", 2)
    (own,) = out_terms(where, [flat, from_core], w_flat, shape, (0,), kind=jnp.float32)
    return (own + beyond.astype(jnp.float32)).astype(jnp.bfloat16)


def fits_head_split(mesh, w_in, gate_gain, dt_bias):
    shards, blocks = mesh.shape["seq"], mesh.shape["head"]
    groups = gate_gain.shape[0] // blocks
    local_heads = dt_bias.shape[0] // blocks
    chans = groups * gate_gain.shape[1] // shards
    return shards == 8 and blocks == 4 and groups == 2 and local_heads % shards == 0 and chans % LANES == 0


def from_behind(shard, axis, by):
    count = lax.axis_size(axis)
    pairs = [(i, i + by) for i in range(count) if 0 <= i + by < count]
    return lax.ppermute(shard, axis, pairs)


def carried_in(shard, axis, combine, identity):
    count, index = (lax.axis_size(axis), lax.axis_index(axis))
    everything = jax.tree.map(
        lambda part, kind: lax.all_gather(part.astype(kind), axis),
        shard,
        (jnp.bfloat16, jnp.bfloat16),
    )
    start = jax.tree.map(
        lambda part, zero: jnp.broadcast_to(jnp.asarray(zero, part.dtype), part.shape),
        shard,
        identity,
    )

    def lap(k, before):
        reached = k < index
        new = combine(
            before, jax.tree.map(lambda part, own: part[k].astype(own.dtype), everything, shard)
        )
        return jax.tree.map(lambda a, b: jnp.where(reached, a, b), new, before)

    return lax.fori_loop(0, count, lap, start)


def normalize(values, gain):
    squares = jnp.mean(values * values, axis=-1, keepdims=True)
    return values * lax.rsqrt(squares + EPS) * gain


def state_block(inputs, step_size, log_decay, in_map, out_map, block_len):
    length = inputs.shape[0]
    stretch_count = length // block_len
    head_count = inputs.shape[1]
    head_size = inputs.shape[2]
    state_size = in_map.shape[1]
    shaped = (
        inputs.reshape(stretch_count, block_len, head_count, head_size),
        step_size.reshape(stretch_count, block_len, head_count),
        log_decay.reshape(stretch_count, block_len, head_count),
        in_map.reshape(stretch_count, block_len, state_size),
        out_map.reshape(stretch_count, block_len, state_size),
    )
    causal = jnp.arange(block_len)[:, None] >= jnp.arange(block_len)[None, :]

    def advance(state_now, pieces):
        stretch_in, stretch_step, stretch_log, stretch_b, stretch_c = pieces
        cumulative = jnp.cumsum(stretch_log, axis=0)
        gap_log = cumulative[:, None, :] - cumulative[None, :, :]
        decays = jnp.where(
            causal[:, :, None], jnp.exp(jnp.where(causal[:, :, None], gap_log, 0.0)), 0.0
        )
        scores = jnp.dot(stretch_c, stretch_b.T, preferred_element_type=jnp.float32)
        wide_c = stretch_c.astype(jnp.float32)
        wide_b = stretch_b.astype(jnp.float32)
        weights = scores[:, :, None] * decays * stretch_step[None, :, :]
        within = jnp.einsum("ijh,jhp->ihp", weights, stretch_in, precision=HIGHEST)
        across = jnp.exp(cumulative)[:, :, None] * jnp.einsum(
            "in,hpn->ihp", wide_c, state_now, precision=HIGHEST
        )
        to_end = jnp.exp(cumulative[-1][None, :] - cumulative) * stretch_step
        fresh_state = jnp.einsum("jh,jhp,jn->hpn", to_end, stretch_in, wide_b, precision=HIGHEST)
        state_next = jnp.exp(cumulative[-1])[:, None, None] * state_now + fresh_state
        return (state_next, within + across)

    start_state = jnp.zeros((head_count, head_size, state_size), jnp.float32)
    final, outputs = lax.scan(advance, start_state, shaped)
    return (outputs.reshape(length, head_count, head_size), final)


def link_states(earlier, later):
    return (earlier[0] + later[0], jnp.exp(later[0])[:, :, None, None] * earlier[1] + later[1])


def sequence_split_body(tokens, norm_gain, w_in, w_dt, dt_bias, a_log, d_skip, conv_w, conv_b, gate_gain, w_out):
    local_rows = tokens.shape[0]
    kernel_len = conv_w.shape[0]
    groups, group_width = gate_gain.shape
    head_count = dt_bias.shape[0]
    per_group = head_count // groups
    head_size = group_width // per_group
    state_size = (conv_b.shape[1] - group_width) // 2
    gathered = lax.all_gather(tokens, "head", axis=1, tiled=True)
    normed = normalize(gathered.astype(jnp.float32), norm_gain).astype(jnp.bfloat16)
    span_rows = normed.shape[0]
    flat_in = w_in.reshape(w_in.shape[0], groups * w_in.shape[2])
    proj_sum = jnp.dot(
        normed,
        lax.all_gather(flat_in, "seq", axis=0, tiled=True),
        preferred_element_type=jnp.float32,
    )
    step_sum = jnp.dot(
        normed, lax.all_gather(w_dt, "seq", axis=0, tiled=True), preferred_element_type=jnp.float32
    )
    projected = proj_sum.astype(jnp.bfloat16).reshape(span_rows, groups, w_in.shape[2])
    step_size = jax.nn.softplus(step_sum + dt_bias[None, :])
    gate_raw = projected[span_rows - local_rows :, :, :group_width]
    own_channels = projected[:, :, group_width:]
    rim_rows = from_behind(own_channels[local_rows - kernel_len + 1 :], "seq", 1)
    extended = jnp.concatenate([rim_rows, own_channels], axis=0)
    summed = conv_b[None, :, :]
    for offset in range(kernel_len):
        summed = summed + conv_w[offset][None, :, :] * extended[
            offset : offset + local_rows
        ].astype(jnp.float32)
    narrow = lax.optimization_barrier(jax.nn.silu(summed).astype(jnp.bfloat16))
    convolved = narrow.astype(jnp.float32)
    inputs = convolved[:, :, :group_width].reshape(local_rows, groups, per_group, head_size)
    in_map = narrow[:, :, group_width : group_width + state_size]
    out_map = narrow[:, :, group_width + state_size :]
    step_grouped = step_size.reshape(local_rows, groups, per_group)
    log_decay = -jnp.exp(a_log).reshape(groups, per_group)[None, :, :] * step_grouped
    run_block = jax.vmap(
        partial(state_block, block_len=STRETCH), in_axes=(1, 1, 1, 1, 1), out_axes=(1, 0)
    )
    local_out, ending = run_block(inputs, step_grouped, log_decay, in_map, out_map)
    totals = jnp.sum(log_decay, axis=0)
    identity = (jnp.zeros_like(totals), jnp.zeros_like(ending))
    prior_decay, incoming = carried_in((totals, ending), "seq", link_states, identity)
    cumulative = jnp.exp(jnp.cumsum(log_decay, axis=0))
    carried = (
        jnp.einsum("tgn,ghpn->tghp", out_map.astype(jnp.float32), incoming, precision=HIGHEST)
        * cumulative[:, :, :, None]
    )
    outputs = local_out + carried + d_skip.reshape(groups, per_group)[None, :, :, None] * inputs
    gated = outputs.reshape(local_rows, groups, group_width) * jax.nn.silu(
        gate_raw.astype(jnp.float32)
    )
    normed_out = normalize(gated, gate_gain[None, :, :]).astype(jnp.bfloat16)
    flat_out = normed_out.reshape(local_rows, groups * group_width)
    terms = jnp.dot(
        flat_out,
        w_out.reshape(groups * group_width, w_out.shape[2]),
        preferred_element_type=jnp.float32,
    )
    return lax.psum_scatter(terms.astype(jnp.bfloat16), "head", scatter_dimension=1, tiled=True)


def solution(mesh):
    in_specs = (
        P("seq", "head"),
        P(),
        P("seq", "head", None),
        P("seq", "head"),
        P("head"),
        P("head"),
        P("head"),
        P(None, "head", None),
        P("head", None),
        P("head", None),
        P("head", None, None),
    )
    out_specs = P("seq", "head")

    def mixer_prefill(*args):
        by_heads = fits_head_split(mesh, args[2], args[9], args[4])
        body = head_split_body if by_heads else sequence_split_body
        mapped = jax.shard_map(
            body, mesh=mesh, in_specs=in_specs, out_specs=out_specs, check_vma=False
        )
        return mapped(*args)

    return mixer_prefill
```

```python
from functools import partial

import jax
import jax.numpy as jnp
from jax import lax
from jax.experimental import pallas as pl
from jax.experimental.pallas import tpu as pltpu
from jax.sharding import PartitionSpec as P

STRETCH = 128


EPS = 1e-05
HIGHEST = lax.Precision.HIGHEST
VMEM_LIMIT = 58 * 1024 * 1024
LANES = 128


def swap(value, axis, bit):
    count = lax.axis_size(axis)
    return lax.ppermute(value, axis, [(i, i ^ bit) for i in range(count)])


def silu_of(v):
    half = 0.5 * v
    return half + half * jnp.tanh(half)


def mixer_kernel(
    cfg,
    where_ref,
    *refs,
):
    (shards, maps_of, parts, dt_rows, blocks, rows, feats, krows, heads, width, state_size, taps, dim) = cfg
    many = shards - 1
    gathered, last = refs[:many], refs[many : many + 2]
    at = many + 2
    mains = []
    for n in parts:
        mains.append(refs[at : at + n])
        at += n
    (map_a, map_b, conv_w, conv_b, dt_bias, neg_rate, skip) = refs[at : at + 7]
    (out_ref, wbuf, dt_all, dt_own, xbuf, pbuf, pnext, cbuf, state, wsem, dsem, xsem) = refs[at + 7 :]
    i = pl.program_id(0)
    steps = pl.num_programs(0)
    me_s, me_h = where_ref[0], where_ref[1]
    chans = heads * width
    conv_cols = chans + 2 * state_size
    main_cols = 2 * chans
    map_cols = 2 * state_size
    per = feats // krows
    map_rows = krows + dt_rows * (krows // (2 * state_size))
    me_q = me_s % (shards // 2)

    def move(copy, start):
        if start:
            copy.start()
        else:
            copy.wait()

    def fetch(step, slot, start):
        which = where_ref[2 + step]
        for k in range(shards // 2):
            for inner in (0, 1):
                @pl.when(which == 2 * k + inner)
                def _(k=k, inner=inner):
                    part = pl.ds(inner * rows, rows)
                    for e in range(blocks):
                        beyond, core = divmod(e, 2)
                        array = k + beyond * (shards // 2)
                        if array < many:
                            src, block = gathered[array].at[core, part, :], e
                        else:
                            src, block = last[core].at[part, :], (e & ~1) + ((me_h & 1) ^ core)
                        dst = xbuf.at[slot, :, pl.ds(pl.multiple_of(block * feats, feats), feats)]
                        move(pltpu.make_async_copy(src, dst, xsem.at[slot, e]), start)

    def weights(start):
        for d in range(shards):
            kb = me_s ^ d
            block = kb // per
            place = ((block // 2) ^ (me_h // 2)) * 2 + (block % 2)
            row = pl.multiple_of(place * feats + (kb % per) * krows, krows)
            source, place_row = maps_of[d]
            map_src = (map_a, map_b)[source]
            lo_row = place_row * map_rows
            depth = krows // len(mains[d])
            for n, src in enumerate(mains[d]):
                dst = wbuf.at[pl.ds(row + n * depth, depth), pl.ds(0, main_cols)]
                move(pltpu.make_async_copy(src, dst, wsem.at[n, d]), start)
            dst = wbuf.at[pl.ds(row, krows), pl.ds(main_cols, map_cols)]
            move(pltpu.make_async_copy(map_src.at[pl.ds(lo_row, krows), :], dst, wsem.at[2, d]), start)
            for n in range(krows // map_cols):
                src = map_src.at[pl.ds(lo_row + krows + n * dt_rows, dt_rows), :]
                dst = dt_all.at[:, pl.ds(pl.multiple_of(row + n * map_cols, map_cols), map_cols)]
                move(pltpu.make_async_copy(src, dst, dsem.at[n, d]), start)

    slot = lax.rem(i, 2)
    shard_count = steps - 1

    @pl.when(i == 0)
    def _():
        fetch(0, 0, True)
        weights(True)
        state[...] = jnp.zeros_like(state)
        cbuf[0:8, :] = jnp.zeros((8, conv_cols), jnp.float32)

    @pl.when(i + 1 < shard_count)
    def _():
        fetch(i + 1, 1 - slot, True)

    @pl.when(i == 0)
    def _():
        weights(False)
        own_row = lax.broadcasted_iota(jnp.int32, (LANES, dt_rows), 0)
        group_row = lax.broadcasted_iota(jnp.int32, (LANES, dt_rows), 1)
        mine = (group_row == own_row + me_q * heads) & (own_row < heads)
        pick = jnp.where(mine, 1.0, 0.0).astype(jnp.bfloat16)
        for lo in range(0, dim, feats):
            dt_own[:, lo : lo + feats] = jnp.dot(
                pick, dt_all[:, lo : lo + feats], preferred_element_type=jnp.float32
            ).astype(jnp.bfloat16)

    @pl.when(i < shard_count)
    def _():
        fetch(i, slot, False)

    total = main_cols + map_cols + LANES
    tiles = [(lo, min(256, total - lo)) for lo in range(0, total, 256)]
    length = STRETCH
    stretches = rows // length

    def row_factor():
        squares = jnp.zeros((rows, LANES), jnp.float32)
        for lo in range(0, dim, LANES):
            part = xbuf[slot, :, lo : lo + LANES].astype(jnp.float32)
            squares = squares + part * part
        squares = jnp.sum(squares, axis=1, keepdims=True)
        return lax.rsqrt(squares * (1.0 / dim) + EPS)

    def project(tile, factor):
        lo, cols = tile
        if lo < total - LANES:
            part = jnp.dot(xbuf[slot], wbuf[:, lo : lo + cols], preferred_element_type=jnp.float32)
        else:
            part = lax.dot_general(
                xbuf[slot], dt_own[...], (((1,), (1,)), ((), ())), preferred_element_type=jnp.float32
            )
        pnext[:, lo : lo + cols] = part * factor

    def hand_over():
        pbuf[:, :chans] = pnext[:, :chans]
        pbuf[:, chans:] = pnext[:, total - LANES :]
        cbuf[8 : 8 + rows, :] = pnext[:, chans : chans + conv_cols]

    def constants():
        tri = lax.broadcasted_iota(jnp.int32, (length, length), 0) >= lax.broadcasted_iota(
            jnp.int32, (length, length), 1
        )
        ones = jnp.where(tri, 1.0, 0.0).astype(jnp.bfloat16)
        row = lax.broadcasted_iota(jnp.int32, (2 * LANES, chans), 0) % LANES
        lane = lax.broadcasted_iota(jnp.int32, (2 * LANES, chans), 1) // width
        widen = jnp.where(row == lane, 1.0, 0.0).astype(jnp.bfloat16)
        lane_head = lax.broadcasted_iota(jnp.int32, (1, chans), 1) // width
        masks = [jnp.where(lane_head == j, 1.0, 0.0).astype(jnp.bfloat16) for j in range(heads)]
        return tri, ones, widen, masks

    def scan(st, tri, ones, widen, masks):
        r0 = st * length
        summed = conv_b[...]
        for k in range(taps):
            first = 8 - (taps - 1) + k + r0
            summed = summed + conv_w[k : k + 1, :] * cbuf[first : first + length, :]
        narrow = silu_of(summed).astype(jnp.bfloat16)
        in_map = narrow[:, chans : chans + state_size]
        out_map = narrow[:, chans + state_size :]
        xf = narrow[:, :chans].astype(jnp.float32)
        raw = pbuf[r0 : r0 + length, chans:] + dt_bias[...]
        step = jnp.maximum(raw, 0.0) + jnp.log1p(jnp.exp(-jnp.abs(raw)))
        logd = neg_rate[...] * step
        term0 = logd.astype(jnp.bfloat16)
        rest = logd - term0.astype(jnp.float32)
        term1 = rest.astype(jnp.bfloat16)
        term2 = (rest - term1.astype(jnp.float32)).astype(jnp.bfloat16)
        sums = jnp.dot(ones, jnp.concatenate([term0, term1, term2], axis=1), preferred_element_type=jnp.float32)
        cum = sums[:, :LANES] + (sums[:, LANES : 2 * LANES] + sums[:, 2 * LANES :])
        cum_t = cum.T
        columns = jnp.concatenate([jnp.exp(cum), step, jnp.exp(cum[length - 1 :, :] - cum)], axis=0)
        high = columns.astype(jnp.bfloat16)
        low = (columns - high.astype(jnp.float32)).astype(jnp.bfloat16)
        wide = jnp.dot(jnp.concatenate([high, low], axis=1), widen, preferred_element_type=jnp.float32)
        since, stepped, to_end = wide[:length], wide[length : 2 * length], wide[2 * length :]
        scores = lax.dot_general(
            out_map, in_map, (((1,), (1,)), ((), ())), preferred_element_type=jnp.float32
        )
        scores = jnp.where(tri, scores, 0.0)
        taken = xf * stepped
        taken_low = taken.astype(jnp.bfloat16)
        weighted, spaced = [], []
        for j in range(heads):
            gap = jnp.minimum(cum[:, j : j + 1] - cum_t[j : j + 1, :], 0.0)
            weighted.append((scores * jnp.exp(gap)).astype(jnp.bfloat16))
            spaced.append(taken_low * masks[j])
        within = jnp.dot(
            jnp.concatenate(weighted, axis=1),
            jnp.concatenate(spaced, axis=0),
            preferred_element_type=jnp.float32,
        )
        now = state[...]
        across = jnp.dot(out_map, now.astype(jnp.bfloat16), preferred_element_type=jnp.float32)
        y = within + since * across + skip[...] * xf
        fresh = lax.dot_general(
            in_map, (taken * to_end).astype(jnp.bfloat16), (((0,), (0,)), ((), ())), preferred_element_type=jnp.float32
        )
        state[...] = since[length - 1 :, :] * now + fresh
        gate = pbuf[r0 : r0 + length, :chans]
        out_ref[r0 : r0 + length, :] = (y * silu_of(gate)).astype(jnp.bfloat16)

    def keep_tail():
        cbuf[0:8, :] = cbuf[rows : rows + 8, :]

    @pl.when(i == 0)
    def _():
        factor = row_factor()
        for tile in tiles:
            project(tile, factor)
        hand_over()

    @pl.when((i > 0) & (i < shard_count))
    def _():
        held = constants()
        factor = row_factor()
        for n in range(max(len(tiles), stretches)):
            if n < len(tiles):
                project(tiles[n], factor)
            if n < stretches:
                scan(n, *held)
        keep_tail()
        hand_over()

    @pl.when(i == shard_count)
    def _():
        held = constants()
        for n in range(stretches):
            scan(n, *held)


def mixer(
    where, gathered, last, mains, maps, maps_of, conv_w, conv_b, dt_bias, neg_rate, skip, rows, heads, width, dim
):
    shards = len(mains)
    feats = last[0].shape[1]
    blocks = dim // feats
    krows = mains[0].shape[0]
    chans = heads * width
    state_size = maps[0].shape[1] // 2
    parts = tuple(len(m) if isinstance(m, tuple) else 1 for m in mains)
    dt_rows = heads * shards // 2
    taps = conv_w.shape[0]
    total = 2 * chans + 2 * state_size + LANES
    cfg = (shards, tuple(maps_of), parts, dt_rows, blocks, rows, feats, krows, heads, width, state_size, taps, dim)
    hbm = pl.BlockSpec(memory_space=pl.ANY)

    def whole(a):
        return pl.BlockSpec(a.shape, lambda i, w: (0,) * a.ndim)

    small = (conv_w, conv_b, dt_bias, neg_rate, skip)
    flat_mains = [part for m in mains for part in (m if isinstance(m, tuple) else (m,))]
    large = (*gathered, *last, *flat_mains, *maps)
    return pl.pallas_call(
        partial(mixer_kernel, cfg),
        out_shape=jax.ShapeDtypeStruct((rows * shards, chans), jnp.bfloat16),
        grid_spec=pltpu.PrefetchScalarGridSpec(
            num_scalar_prefetch=1,
            grid=(shards + 1,),
            in_specs=[hbm] * len(large) + [whole(a) for a in small],
            out_specs=pl.BlockSpec((rows, chans), lambda i, w: (jnp.maximum(i - 1, 0), 0)),
            scratch_shapes=[
                pltpu.VMEM((dim, total - LANES), jnp.bfloat16),
                pltpu.VMEM((dt_rows, dim), jnp.bfloat16),
                pltpu.VMEM((LANES, dim), jnp.bfloat16),
                pltpu.VMEM((2, rows, dim), jnp.bfloat16),
                pltpu.VMEM((rows, chans + LANES), jnp.float32),
                pltpu.VMEM((rows, total), jnp.float32),
                pltpu.VMEM((8 + rows, chans + 2 * state_size), jnp.float32),
                pltpu.VMEM((state_size, chans), jnp.float32),
                pltpu.SemaphoreType.DMA((3, shards)),
                pltpu.SemaphoreType.DMA((krows // (2 * state_size), shards)),
                pltpu.SemaphoreType.DMA((2, blocks)),
            ],
        ),
        compiler_params=pltpu.CompilerParams(vmem_limit_bytes=VMEM_LIMIT, dimension_semantics=("arbitrary",)),
        cost_estimate=pl.CostEstimate(
            flops=2 * rows * shards * dim * total, bytes_accessed=2 * rows * shards * dim, transcendentals=0
        ),
    )(where, *large, *small)


def terms_kernel(cfg, where_ref, *refs):
    shards, chans, groups, order, keep, added = cfg
    count = shards + 1 if keep else 1 + added
    values, w_hbm, outs = refs[:count], refs[count], refs[count + 1 : count + 1 + len(order)]
    w_buf, sem = refs[-2], refs[-1]
    flat = refs[count + 1 + len(order)] if keep else values[0]
    depth, feats = w_buf.shape[1:]
    chunks = sem.shape[1]
    part_rows = depth // chunks
    me_s = where_ref[0]

    def copy(block, n):
        part = pl.ds(n * part_rows, part_rows)
        lane = pl.multiple_of((where_ref[1] ^ order[block]) * feats, feats)
        return pltpu.make_async_copy(
            w_hbm.at[part, pl.ds(lane, feats)], w_buf.at[block, part, :], sem.at[block, n]
        )

    for block in range(len(order)):
        for n in range(chunks):
            copy(block, n).start()
    if keep:
        gated, gain = values[:shards], values[shards]
        per = shards // groups
        for g in range(groups):
            squares = 0.0
            parts = []
            for d in range(g * per, (g + 1) * per):
                part = gated[d][...].astype(jnp.float32)
                parts.append(part)
                squares = squares + jnp.sum(part * part, axis=1, keepdims=True)
            factor = lax.rsqrt(squares * (1.0 / (per * chans)) + EPS)
            for d, part in zip(range(g * per, (g + 1) * per), parts):
                t = me_s ^ d
                value = (part * factor * gain[pl.ds(t, 1), :]).astype(jnp.bfloat16)
                flat[:, pl.ds(pl.multiple_of(t * chans, chans), chans)] = value
    for block, out_ref in enumerate(outs):
        for n in range(chunks):
            copy(block, n).wait()
        for lo in range(0, feats, 256):
            cols = min(256, feats - lo)
            part = jnp.dot(flat[...], w_buf[block, :, lo : lo + cols], preferred_element_type=jnp.float32)
            if added:
                part = part + values[1][:, lo : lo + cols].astype(jnp.float32)
            out_ref[:, lo : lo + cols] = part.astype(out_ref.dtype)


def out_terms(where, values, w_flat, shape, order, keep=False, kind=jnp.bfloat16):
    shards, groups, rows, chans, blocks = shape
    depth, dim = w_flat.shape
    feats = dim // blocks
    vmem = pl.BlockSpec(memory_space=pltpu.VMEM)
    widths = [feats] * len(order) + ([depth] if keep else [])
    added = 0 if keep else len(values) - 1
    out_shape = tuple(jax.ShapeDtypeStruct((rows, n), kind) for n in widths)
    return pl.pallas_call(
        partial(terms_kernel, (shards, chans, groups, order, keep, added)),
        out_shape=out_shape,
        in_specs=[pl.BlockSpec(memory_space=pltpu.SMEM)] + [vmem] * len(values) + [pl.BlockSpec(memory_space=pl.ANY)],
        out_specs=(vmem,) * len(widths),
        scratch_shapes=[
            pltpu.VMEM((len(order), depth, feats), jnp.bfloat16),
            pltpu.SemaphoreType.DMA((len(order), 8)),
        ],
        compiler_params=pltpu.CompilerParams(vmem_limit_bytes=VMEM_LIMIT),
        cost_estimate=pl.CostEstimate(
            flops=rows * feats,
            bytes_accessed=rows * feats,
            transcendentals=0,
        ),
    )(where, *values, w_flat)


def line(value, pairs):
    return lax.ppermute(value, "seq", [(2 * a + y, 2 * b + y) for a, b in pairs for y in (0, 1)])


def stack(*parts):
    return jnp.concatenate(parts, axis=0)


def both_cores(value):
    pairs = [[i, i + 1] for i in range(0, lax.axis_size("head"), 2)]
    return lax.all_gather(value, "head", axis=0, axis_index_groups=pairs)


def together(*values):
    return lax.optimization_barrier(values)


def exchange(tokens, w_in, weights_of):
    at = lax.axis_index("seq") // 2
    middle = (at == 1) | (at == 2)
    cross, outward = [(1, 2), (2, 1)], [(1, 0), (2, 3)]

    def x_swap(v):
        return swap(v, "head", 2)

    def s_swap(v, bit):
        return swap(v, "seq", bit)

    xp, y0, z1, c0, (m1, m7, far_map), w_in = together(
        x_swap(tokens),
        s_swap(tokens, 1),
        s_swap(tokens, 2),
        line(tokens, cross),
        weights_of(w_in, (1, 7, "far")),
        w_in,
    )
    xy, yz1, c1, o0, (m2, m6, m5, m4, m3, m0, own_map) = together(
        x_swap(y0),
        s_swap(z1, 1),
        line(z1, cross),
        line(c0, outward),
        weights_of(w_in, (2, 6, 5, 4, 3, 0, "own")),
    )
    q1 = jnp.where(middle, c0, o0)
    q1, z1, yz1, c1, m7, far_map, m1 = together(q1, z1, yz1, c1, m7, far_map, m1)
    xz1, xyz1, w1, w7, yq1, o1, far_map = together(
        x_swap(z1), x_swap(yz1), s_swap(m1, 1), s_swap(m7, 7), s_swap(q1, 1), line(c1, outward), s_swap(far_map, 4)
    )
    own = [stack(tokens, y0), stack(z1, yz1)]
    across = [stack(xp, xy), stack(xz1, xyz1)]
    q2 = jnp.where(middle, c1, o1)
    maps = stack(own_map, far_map)
    half = m6.shape[0] // 2
    q2, q1, yq1, maps, m5, m6a, m6b, m2 = together(q2, q1, yq1, maps, m5, m6[:half], m6[half:], m2)
    xq1, xyq1, w2, w5, w6a, yq2, maps_z = together(
        x_swap(q1), x_swap(yq1), s_swap(m2, 2), s_swap(m5, 5), s_swap(m6a, 6), s_swap(q2, 1), s_swap(maps, 2)
    )
    maps = stack(maps, maps_z)
    q2, yq2, maps, m4, m6b, m3 = together(q2, yq2, maps, m4, m6b, m3)
    xq2, xyq2, w4, w6b, maps_y, w3 = together(
        x_swap(q2), x_swap(yq2), s_swap(m4, 4), s_swap(m6b, 6), s_swap(maps, 1), s_swap(m3, 3)
    )
    own += [stack(q1, yq1), stack(q2, yq2)]
    across += [stack(xq1, xyq1)]
    xa3 = stack(xq2, xyq2)
    gathered = [both_cores(v) for v in own + across]
    last = (xa3, swap(xa3, "head", 1))
    mains = [m0, w1, w2, w3, w4, w5, (w6a, w6b), w7]
    place = {0: 0, 4: 1, 2: 2, 6: 3}
    maps_of = [(d & 1, place[d & ~1]) for d in range(8)]
    return gathered, last, mains, (maps, maps_y), maps_of


def piece_table(shards):
    me = lax.axis_index("seq")
    shard = jnp.arange(shards)
    outer = (shard // 2) ^ (me // 2)
    middle = (me // 2 == 1) | (me // 2 == 2)
    slot = jnp.where((outer >= 2) & middle, outer ^ 1, outer)
    return slot * 2 + ((shard ^ me) & 1)


def head_split_body(
    tokens, norm_gain, w_in, w_dt, dt_bias, a_log, d_skip, conv_w, conv_b, gate_gain, w_out
):
    shards, blocks = lax.axis_size("seq"), lax.axis_size("head")
    s, h = lax.axis_index("seq"), lax.axis_index("head")
    rows = tokens.shape[0]
    krows, groups, wide = w_in.shape
    group_width = gate_gain.shape[1]
    state_size = (conv_b.shape[1] - group_width) // 2
    local_heads = dt_bias.shape[0]
    heads = local_heads // shards
    width = groups * group_width // local_heads
    chans = heads * width
    per = shards // groups
    dim = krows * shards

    gain = lax.dynamic_slice_in_dim(norm_gain, s * krows, krows, 0)

    dt_cols = local_heads // groups

    def weights_of(w_in, names):
        def columns(t, first, count):
            part = lax.dynamic_slice(w_in, (0, t // per, first), (krows, 1, count))[:, 0]
            return (part.astype(jnp.float32) * gain[:, None]).astype(jnp.bfloat16)

        def one(name):
            if name in ("far", "own"):
                t = s ^ per if name == "far" else s
                dt = lax.dynamic_slice_in_dim(w_dt, (t // per) * dt_cols, dt_cols, 1).T
                dt = (dt.astype(jnp.float32) * gain[None, :]).astype(jnp.bfloat16)
                cols = 2 * state_size
                rows_of_dt = [dt[:, lo : lo + cols] for lo in range(0, krows, cols)]
                return jnp.concatenate([columns(t, 2 * group_width, cols), *rows_of_dt], axis=0)
            t = s ^ name
            first = (t % per) * chans
            return jnp.concatenate(
                [columns(t, first, chans), columns(t, group_width + first, chans)], axis=1
            )

        return tuple(one(name) for name in names)

    gathered, last, mains, maps, maps_of = exchange(tokens, w_in, weights_of)

    group = s // per
    quarter = (s % per) * chans

    def own_channels(a):
        a = lax.dynamic_index_in_dim(a, group, a.ndim - 2, keepdims=False)
        inputs = lax.dynamic_slice_in_dim(a, quarter, chans, a.ndim - 1)
        return jnp.concatenate([inputs, a[..., group_width:]], axis=-1)

    def own_heads(a):
        return lax.dynamic_slice_in_dim(a, s * heads, heads, 0)

    def lanes(a):
        return jnp.pad(a, (0, LANES - heads))[None, :]

    where = jnp.concatenate([jnp.stack([s, h]), piece_table(shards)]).astype(jnp.int32)
    gated = mixer(
        where,
        gathered,
        last,
        mains,
        maps,
        maps_of,
        own_channels(conv_w),
        own_channels(conv_b)[None, :],
        lanes(own_heads(dt_bias)),
        lanes(-jnp.exp(own_heads(a_log))),
        jnp.repeat(own_heads(d_skip), width)[None, :],
        rows,
        heads,
        width,
        dim,
    )
    blocks_out = [
        lax.dynamic_slice_in_dim(gated, (s ^ d) * rows, rows, 0) for d in range(shards)
    ]
    arrived = [blocks_out[0]] + [None] * (shards - 1)
    for d in range(shards - 1, 0, -1):
        arrived[d] = swap(blocks_out[d], "seq", d)

    gains = gate_gain.reshape(shards, chans)
    w_flat = w_out.reshape(groups * group_width, w_out.shape[2])
    shape = (shards, groups, rows, chans, blocks)
    shape = (shards, groups, rows, chans, blocks)
    first, third, flat = out_terms(where, [*arrived, gains], w_flat, shape, (3, 1), True)
    via_core, from_core = swap(first, "head", 1), swap(third, "head", 1)
    (to_pair,) = out_terms(where, [flat, via_core], w_flat, shape, (2,))
    to_pair, flat = together(to_pair, flat)
    beyond = swap(to_pair, "head", 2)
    (own,) = out_terms(where, [flat, from_core], w_flat, shape, (0,), kind=jnp.float32)
    return (own + beyond.astype(jnp.float32)).astype(jnp.bfloat16)


def fits_head_split(mesh, w_in, gate_gain, dt_bias):
    shards, blocks = mesh.shape["seq"], mesh.shape["head"]
    groups = gate_gain.shape[0] // blocks
    local_heads = dt_bias.shape[0] // blocks
    chans = groups * gate_gain.shape[1] // shards
    return shards == 8 and blocks == 4 and groups == 2 and local_heads % shards == 0 and chans % LANES == 0


def from_behind(shard, axis, by):
    count = lax.axis_size(axis)
    pairs = [(i, i + by) for i in range(count) if 0 <= i + by < count]
    return lax.ppermute(shard, axis, pairs)


def carried_in(shard, axis, combine, identity):
    count, index = (lax.axis_size(axis), lax.axis_index(axis))
    everything = jax.tree.map(
        lambda part, kind: lax.all_gather(part.astype(kind), axis),
        shard,
        (jnp.bfloat16, jnp.bfloat16),
    )
    start = jax.tree.map(
        lambda part, zero: jnp.broadcast_to(jnp.asarray(zero, part.dtype), part.shape),
        shard,
        identity,
    )

    def lap(k, before):
        reached = k < index
        new = combine(
            before, jax.tree.map(lambda part, own: part[k].astype(own.dtype), everything, shard)
        )
        return jax.tree.map(lambda a, b: jnp.where(reached, a, b), new, before)

    return lax.fori_loop(0, count, lap, start)


def normalize(values, gain):
    squares = jnp.mean(values * values, axis=-1, keepdims=True)
    return values * lax.rsqrt(squares + EPS) * gain


def state_block(inputs, step_size, log_decay, in_map, out_map, block_len):
    length = inputs.shape[0]
    stretch_count = length // block_len
    head_count = inputs.shape[1]
    head_size = inputs.shape[2]
    state_size = in_map.shape[1]
    shaped = (
        inputs.reshape(stretch_count, block_len, head_count, head_size),
        step_size.reshape(stretch_count, block_len, head_count),
        log_decay.reshape(stretch_count, block_len, head_count),
        in_map.reshape(stretch_count, block_len, state_size),
        out_map.reshape(stretch_count, block_len, state_size),
    )
    causal = jnp.arange(block_len)[:, None] >= jnp.arange(block_len)[None, :]

    def advance(state_now, pieces):
        stretch_in, stretch_step, stretch_log, stretch_b, stretch_c = pieces
        cumulative = jnp.cumsum(stretch_log, axis=0)
        gap_log = cumulative[:, None, :] - cumulative[None, :, :]
        decays = jnp.where(
            causal[:, :, None], jnp.exp(jnp.where(causal[:, :, None], gap_log, 0.0)), 0.0
        )
        scores = jnp.dot(stretch_c, stretch_b.T, preferred_element_type=jnp.float32)
        wide_c = stretch_c.astype(jnp.float32)
        wide_b = stretch_b.astype(jnp.float32)
        weights = scores[:, :, None] * decays * stretch_step[None, :, :]
        within = jnp.einsum("ijh,jhp->ihp", weights, stretch_in, precision=HIGHEST)
        across = jnp.exp(cumulative)[:, :, None] * jnp.einsum(
            "in,hpn->ihp", wide_c, state_now, precision=HIGHEST
        )
        to_end = jnp.exp(cumulative[-1][None, :] - cumulative) * stretch_step
        fresh_state = jnp.einsum("jh,jhp,jn->hpn", to_end, stretch_in, wide_b, precision=HIGHEST)
        state_next = jnp.exp(cumulative[-1])[:, None, None] * state_now + fresh_state
        return (state_next, within + across)

    start_state = jnp.zeros((head_count, head_size, state_size), jnp.float32)
    final, outputs = lax.scan(advance, start_state, shaped)
    return (outputs.reshape(length, head_count, head_size), final)


def link_states(earlier, later):
    return (earlier[0] + later[0], jnp.exp(later[0])[:, :, None, None] * earlier[1] + later[1])


def sequence_split_body(tokens, norm_gain, w_in, w_dt, dt_bias, a_log, d_skip, conv_w, conv_b, gate_gain, w_out):
    local_rows = tokens.shape[0]
    kernel_len = conv_w.shape[0]
    groups, group_width = gate_gain.shape
    head_count = dt_bias.shape[0]
    per_group = head_count // groups
    head_size = group_width // per_group
    state_size = (conv_b.shape[1] - group_width) // 2
    gathered = lax.all_gather(tokens, "head", axis=1, tiled=True)
    normed = normalize(gathered.astype(jnp.float32), norm_gain).astype(jnp.bfloat16)
    span_rows = normed.shape[0]
    flat_in = w_in.reshape(w_in.shape[0], groups * w_in.shape[2])
    proj_sum = jnp.dot(
        normed,
        lax.all_gather(flat_in, "seq", axis=0, tiled=True),
        preferred_element_type=jnp.float32,
    )
    step_sum = jnp.dot(
        normed, lax.all_gather(w_dt, "seq", axis=0, tiled=True), preferred_element_type=jnp.float32
    )
    projected = proj_sum.astype(jnp.bfloat16).reshape(span_rows, groups, w_in.shape[2])
    step_size = jax.nn.softplus(step_sum + dt_bias[None, :])
    gate_raw = projected[span_rows - local_rows :, :, :group_width]
    own_channels = projected[:, :, group_width:]
    rim_rows = from_behind(own_channels[local_rows - kernel_len + 1 :], "seq", 1)
    extended = jnp.concatenate([rim_rows, own_channels], axis=0)
    summed = conv_b[None, :, :]
    for offset in range(kernel_len):
        summed = summed + conv_w[offset][None, :, :] * extended[
            offset : offset + local_rows
        ].astype(jnp.float32)
    narrow = lax.optimization_barrier(jax.nn.silu(summed).astype(jnp.bfloat16))
    convolved = narrow.astype(jnp.float32)
    inputs = convolved[:, :, :group_width].reshape(local_rows, groups, per_group, head_size)
    in_map = narrow[:, :, group_width : group_width + state_size]
    out_map = narrow[:, :, group_width + state_size :]
    step_grouped = step_size.reshape(local_rows, groups, per_group)
    log_decay = -jnp.exp(a_log).reshape(groups, per_group)[None, :, :] * step_grouped
    run_block = jax.vmap(
        partial(state_block, block_len=STRETCH), in_axes=(1, 1, 1, 1, 1), out_axes=(1, 0)
    )
    local_out, ending = run_block(inputs, step_grouped, log_decay, in_map, out_map)
    totals = jnp.sum(log_decay, axis=0)
    identity = (jnp.zeros_like(totals), jnp.zeros_like(ending))
    prior_decay, incoming = carried_in((totals, ending), "seq", link_states, identity)
    cumulative = jnp.exp(jnp.cumsum(log_decay, axis=0))
    carried = (
        jnp.einsum("tgn,ghpn->tghp", out_map.astype(jnp.float32), incoming, precision=HIGHEST)
        * cumulative[:, :, :, None]
    )
    outputs = local_out + carried + d_skip.reshape(groups, per_group)[None, :, :, None] * inputs
    gated = outputs.reshape(local_rows, groups, group_width) * jax.nn.silu(
        gate_raw.astype(jnp.float32)
    )
    normed_out = normalize(gated, gate_gain[None, :, :]).astype(jnp.bfloat16)
    flat_out = normed_out.reshape(local_rows, groups * group_width)
    terms = jnp.dot(
        flat_out,
        w_out.reshape(groups * group_width, w_out.shape[2]),
        preferred_element_type=jnp.float32,
    )
    return lax.psum_scatter(terms.astype(jnp.bfloat16), "head", scatter_dimension=1, tiled=True)


def solution(mesh):
    in_specs = (
        P("seq", "head"),
        P(),
        P("seq", "head", None),
        P("seq", "head"),
        P("head"),
        P("head"),
        P("head"),
        P(None, "head", None),
        P("head", None),
        P("head", None),
        P("head", None, None),
    )
    out_specs = P("seq", "head")

    def mixer_prefill(*args):
        by_heads = fits_head_split(mesh, args[2], args[9], args[4])
        body = head_split_body if by_heads else sequence_split_body
        mapped = jax.shard_map(
            body, mesh=mesh, in_specs=in_specs, out_specs=out_specs, check_vma=False
        )
        return mapped(*args)

    return mixer_prefill
```
